128 devices in a mesh: along: 16 (over y, x), across: 8 (over z, core).
Axes of the slice: x: 4, y: 4, z: 4, core: 2. Of those that a mesh axis runs over, the one named last changes fastest.
Arguments:
- populations: float32 [19, 512, 256, 128], P(None, 'along', 'across')
- link_cell: int32 [16, 8, 8192], P('along', 'across'), may hold values from 0 to 131071, as said below
- link_dir: int32 [16, 8, 8192], P('along', 'across'), may hold values from 1 to 18
- link_floe: int32 [16, 8, 8192], P('along', 'across'), may hold values from -1 to 262143, as said below
- floe_place: float32 [3, 262144], P(None, ('along', 'across')), may hold values from 0 to 1
- floe_velocity: float32 [6, 262144], P(None, ('along', 'across')), may hold values from -1 to 1
- floe_response: float32 [2, 262144], P(None, ('along', 'across')), may hold values from 0.5 to 5
Outputs:
- relaxed: float32 [19, 512, 256, 128], P(None, 'along', 'across')
- floe_motion: float32 [6, 262144], P(None, ('along', 'across'))
The draws below stay inside these ranges and needn't reach their ends.
Inputs may be any that keep to these rules, and one draw needn't show every extreme that they name: `link_cell`: within one block the cell numbers of all slots are distinct. `link_floe`: -1 marks an empty slot; a link's floe is owned by a block at most one block away along and across, counting around the ends; some block has no empty slot.
All inputs are finite; a program needn't handle non-finite values.
Results may differ from the reference program's by a relative error of at most 0.00005.
Values sent between devices are 32-bit elements; how exact they have to be, the bound alone decides.
No kernel may reach another device: no remote copies, remote signals or barrier semaphores. Data moves between devices by JAX's collectives and lax.ppermute only.
A program may use at most 256 MiB of HBM per device.

```python
import math
import jax
import jax.numpy as jnp

CX = 32
CY = 32
NZ = 128
LINKS = 8192
FLOE_DEV = 2048
NX = 512
NY = 256
FLOES = 262144
N_ALONG = 16
N_ACROSS = 8


DIRECTIONS = [(0, 0, 0), (0, 0, 1), (0, 0, -1), (1, 0, 0), (-1, 0, 0), (0, 1, 0), (0, -1, 0), (1, 1, 0), (-1, -1, 0), (1, -1, 0), (-1, 1, 0), (1, 0, 1), (-1, 0, -1), (1, 0, -1), (-1, 0, 1), (0, 1, 1), (0, -1, -1), (0, 1, -1), (0, -1, 1)]


WEIGHTS = [1.0 / 3.0] + [1.0 / 18.0] * 6 + [1.0 / 36.0] * 12


def draw_populations(key, part):
    base = jax.random.fold_in(key, 11)
    subkeys = jax.random.split(base, 2)
    flow_field = jax.random.uniform(subkeys[0], (3, NX, NY, NZ), jnp.float32, -0.05, 0.05)
    jitter = jax.random.uniform(subkeys[1], (19, NX, NY, NZ), jnp.float32, 0.9, 1.1)
    rows = []
    for i in range(19):
        step_x, step_y, step_z = DIRECTIONS[i]
        projection = step_x * flow_field[0] + step_y * flow_field[1] + step_z * flow_field[2]
        rows.append(WEIGHTS[i] * jitter[i] * (1.0 + 3.0 * projection))
    return jnp.stack(rows).astype(jnp.float32)


def link_table(key):
    base = jax.random.fold_in(key, 23)
    subkeys = jax.random.split(base, 8)
    block_count = N_ALONG * N_ACROSS
    shape = (N_ALONG, N_ACROSS, LINKS)
    cell_keys = jax.random.split(subkeys[0], block_count)
    cell_index = jax.vmap(lambda single: jax.random.permutation(single, CX * CY * NZ)[:LINKS])(cell_keys)
    cell_index = cell_index.reshape(shape).astype(jnp.int32)
    direction = jax.random.randint(subkeys[1], shape, 1, 19).astype(jnp.int32)
    filled = jax.random.randint(subkeys[2], (block_count,), 3 * LINKS // 10, LINKS + 1)
    full_block = jax.random.randint(subkeys[3], (), 0, block_count)
    block_ids = jnp.arange(block_count, dtype=jnp.int32)
    filled = jnp.where(block_ids == full_block, LINKS, filled)
    filled = jnp.where(block_ids == (full_block + 1) % block_count, 3 * LINKS // 10, filled)
    filled = filled.reshape(N_ALONG, N_ACROSS, 1)
    slot_index = jnp.arange(LINKS, dtype=jnp.int32)[None, None, :]
    active = slot_index < filled
    step_along = jax.random.randint(subkeys[4], shape, -1, 2)
    step_across = jax.random.randint(subkeys[5], shape, -1, 2)
    member = jax.random.randint(subkeys[6], shape, 0, FLOE_DEV)
    along_rows = jnp.arange(N_ALONG, dtype=jnp.int32)[:, None, None]
    across_rows = jnp.arange(N_ACROSS, dtype=jnp.int32)[None, :, None]
    owner_along = (along_rows + step_along) % N_ALONG
    owner_across = (across_rows + step_across) % N_ACROSS
    floe_id = (owner_along * N_ACROSS + owner_across) * FLOE_DEV + member
    final_slot = (along_rows == N_ALONG - 1) & (across_rows == N_ACROSS - 1) & (slot_index == 0)
    floe_id = jnp.where(final_slot, FLOES - 1, floe_id)
    floe_id = jnp.where(active, floe_id, -1).astype(jnp.int32)
    return (cell_index, direction, floe_id)


def draw_link_cell(key, part):
    return link_table(key)[0]


def draw_link_dir(key, part):
    return link_table(key)[1]


def draw_link_floe(key, part):
    return link_table(key)[2]


def levels(own_key, shape, cuts, least, top_value):
    level = 1.0
    for position, parts in cuts:
        steps = jax.random.uniform(jax.random.fold_in(jax.random.fold_in(own_key, 6), position), (parts,), jnp.float32, least / len(cuts), top_value / len(cuts))
        level = level * jnp.repeat(jnp.exp(steps), shape[position] // parts).reshape((-1,) + (1,) * (len(shape) - 1 - position))
    return level


def setup_inputs(seed: int = 0) -> dict:
    key_list = jax.random.split(jax.random.key(seed), 8)
    return {
        "populations": draw_populations(jax.random.fold_in(key_list[7], 71), 0),
        "link_cell": draw_link_cell(jax.random.fold_in(key_list[7], 71), 0),
        "link_dir": draw_link_dir(jax.random.fold_in(key_list[7], 71), 0),
        "link_floe": draw_link_floe(jax.random.fold_in(key_list[7], 71), 0),
        "floe_place": jnp.clip(1.0 * jax.random.uniform(key_list[4], (3, FLOES), jnp.float32) ** levels(key_list[4], (3, FLOES), ((1, 128),), -0.2, 0.2), 0.0, 1.0),
        "floe_velocity": jnp.clip(jax.random.uniform(key_list[5], (6, FLOES), jnp.float32, -1.0, 1.0) * levels(key_list[5], (6, FLOES), ((1, 128),), -0.4, 0.0), -1.0, 1.0),
        "floe_response": jnp.clip(jnp.exp(math.log(5.0) - 2.3025851 * jax.random.uniform(key_list[6], (2, FLOES), jnp.float32) ** levels(key_list[6], (2, FLOES), ((1, 128),), -0.2, 0.2)), 0.5, 5.0),
    }


DIRECTIONS = [(0, 0, 0), (0, 0, 1), (0, 0, -1), (1, 0, 0), (-1, 0, 0), (0, 1, 0), (0, -1, 0),
              (1, 1, 0), (-1, -1, 0), (1, -1, 0), (-1, 1, 0), (1, 0, 1), (-1, 0, -1),
              (1, 0, -1), (-1, 0, 1), (0, 1, 1), (0, -1, -1), (0, 1, -1), (0, -1, 1)]
WEIGHTS = [1.0 / 3.0] + [1.0 / 18.0] * 6 + [1.0 / 36.0] * 12
RELAXATION = 1.0 / 0.6
FLOW_SCALE = 0.02
LEVER_SCALE = 64.0


def opposite(i):
    if i == 0:
        return 0
    return i + 1 if i % 2 == 1 else i - 1


def cross_product(first, second):
    return jnp.stack([first[1] * second[2] - first[2] * second[1],
                      first[2] * second[0] - first[0] * second[2],
                      first[0] * second[1] - first[1] * second[0]])


def pull_plane(shifted, own_back, step_z):
    if step_z == 1:
        return jnp.concatenate([own_back[..., :1], shifted[..., :-1]], axis=-1)
    if step_z == -1:
        return jnp.concatenate([shifted[..., 1:], own_back[..., -1:]], axis=-1)
    return shifted


def collide(bounded):
    density = bounded[0]
    momentum_x = bounded[0] * 0.0
    momentum_y = bounded[0] * 0.0
    momentum_z = bounded[0] * 0.0
    for i in range(1, 19):
        density = density + bounded[i]
    for i in range(19):
        step_x, step_y, step_z = DIRECTIONS[i]
        if step_x != 0:
            momentum_x = momentum_x + step_x * bounded[i]
        if step_y != 0:
            momentum_y = momentum_y + step_y * bounded[i]
        if step_z != 0:
            momentum_z = momentum_z + step_z * bounded[i]
    velocity_x = momentum_x / density
    velocity_y = momentum_y / density
    velocity_z = momentum_z / density
    speed_square = velocity_x * velocity_x + velocity_y * velocity_y + velocity_z * velocity_z
    relaxed_list = []
    for i in range(19):
        step_x, step_y, step_z = DIRECTIONS[i]
        projection = step_x * velocity_x + step_y * velocity_y + step_z * velocity_z
        equilibrium = WEIGHTS[i] * density * (1.0 + 3.0 * projection + 4.5 * projection * projection - 1.5 * speed_square)
        relaxed_list.append(bounded[i] - RELAXATION * (bounded[i] - equilibrium))
    return jnp.stack(relaxed_list)


def lever_of(reach_along, reach_across, local_x, local_y, local_z, heading, floe_state, width_x, width_y, depth):
    arm_x = -reach_along.astype(jnp.float32) * width_x + local_x.astype(jnp.float32) + 0.5 * heading[0] - floe_state[0] * width_x
    arm_y = -reach_across.astype(jnp.float32) * width_y + local_y.astype(jnp.float32) + 0.5 * heading[1] - floe_state[1] * width_y
    arm_z = local_z.astype(jnp.float32) + 0.5 * heading[2] - floe_state[2] * depth
    return jnp.stack([arm_x, arm_y, arm_z])


def link_effect(f_here, heading, weight, lever_arm, floe_state):
    rotation = cross_product(floe_state[6:9], lever_arm)
    wall_speed = FLOW_SCALE * (floe_state[3:6] + rotation / LEVER_SCALE)
    normal_speed = heading[0] * wall_speed[0] + heading[1] * wall_speed[1] + heading[2] * wall_speed[2]
    returned = f_here - 6.0 * weight * normal_speed
    impulse = heading * (f_here + returned)
    torque = cross_product(lever_arm, impulse)
    return returned, impulse, torque


def reference(populations, link_cell, link_dir, link_floe, floe_place, floe_velocity, floe_response):
    read_list = []
    for i in range(19):
        step_x, step_y, step_z = DIRECTIONS[i]
        shifted = jnp.roll(populations[i], (step_x, step_y), axis=(0, 1))
        read_list.append(pull_plane(shifted, populations[opposite(i)], step_z))
    read = jnp.stack(read_list)

    along_grid = jnp.broadcast_to(jnp.arange(N_ALONG, dtype=jnp.int32)[:, None, None], link_cell.shape).reshape(-1)
    across_grid = jnp.broadcast_to(jnp.arange(N_ACROSS, dtype=jnp.int32)[None, :, None], link_cell.shape).reshape(-1)
    cell_index = link_cell.reshape(-1)
    direction = link_dir.reshape(-1)
    floe_id = link_floe.reshape(-1)
    active = floe_id >= 0
    floe_index = jnp.maximum(floe_id, 0)
    owner_block = floe_index // FLOE_DEV
    owner_along = owner_block // N_ACROSS
    owner_across = owner_block % N_ACROSS
    reach_along = (owner_along - along_grid + 1) % N_ALONG - 1
    reach_across = (owner_across - across_grid + 1) % N_ACROSS - 1
    local_x = cell_index // (CY * NZ)
    local_y = (cell_index // NZ) % CY
    local_z = cell_index % NZ
    global_x = along_grid * CX + local_x
    global_y = across_grid * CY + local_y
    vectors = jnp.array(DIRECTIONS, dtype=jnp.float32)
    heading = vectors[direction].T
    weight = jnp.array(WEIGHTS, dtype=jnp.float32)[direction]
    floe_state = jnp.concatenate([floe_place, floe_velocity], axis=0)[:, floe_index]
    f_here = populations[direction, global_x, global_y, local_z]
    lever_arm = lever_of(reach_along, reach_across, local_x, local_y, local_z, heading, floe_state, CX, CY, NZ)
    returned, impulse, torque = link_effect(f_here, heading, weight, lever_arm, floe_state)
    reverse = jnp.where(direction % 2 == 1, direction + 1, direction - 1)
    sentinel = 19 * NX * NY * NZ
    targets = jnp.where(active, ((reverse * NX + global_x) * NY + global_y) * NZ + local_z, sentinel)
    bounded = read.reshape(-1).at[targets].set(returned, mode="drop").reshape(read.shape)
    relaxed = collide(bounded)

    link_loads = jnp.concatenate([impulse, torque], axis=0) * active.astype(jnp.float32)
    loads = jax.ops.segment_sum(link_loads.T, floe_index, num_segments=FLOES).T
    floe_motion = jnp.concatenate([floe_velocity[0:3] + floe_response[0] * loads[0:3],
                                   floe_velocity[3:6] + floe_response[1] * loads[3:6] / LEVER_SCALE], axis=0)
    return relaxed, floe_motion
```

```python
import functools

import jax
import jax.numpy as jnp
from jax import lax
from jax.experimental import pallas as pl
from jax.experimental.pallas import tpu as pltpu
from jax.sharding import PartitionSpec as P

DIRECTIONS = [
    (0, 0, 0),
    (0, 0, 1),
    (0, 0, -1),
    (1, 0, 0),
    (-1, 0, 0),
    (0, 1, 0),
    (0, -1, 0),
    (1, 1, 0),
    (-1, -1, 0),
    (1, -1, 0),
    (-1, 1, 0),
    (1, 0, 1),
    (-1, 0, -1),
    (1, 0, -1),
    (-1, 0, 1),
    (0, 1, 1),
    (0, -1, -1),
    (0, 1, -1),
    (0, -1, 1),
]
WEIGHTS = [1.0 / 3.0] + [1.0 / 18.0] * 6 + [1.0 / 36.0] * 12
RELAXATION = 1.0 / 0.6
FLOW_SCALE = 0.02
LEVER_SCALE = 64.0

WX = 32
WY = 32
NZ = 128
COLUMNS = WX * WY
MEMBERS = 2048
GROUPS = MEMBERS // 128
STATE_ROWS = 6 * GROUPS
FACE = 5 * WX
EDGE_ROWS = 8
CHUNK = 1024

X_UP = [i for i in range(19) if DIRECTIONS[i][0] == 1]
X_DOWN = [i for i in range(19) if DIRECTIONS[i][0] == -1]
Y_UP = [i for i in range(19) if DIRECTIONS[i][1] == 1]
Y_DOWN = [i for i in range(19) if DIRECTIONS[i][1] == -1]

VMEM_LIMIT = 58 * 1024 * 1024


def opposite(i):
    if i == 0:
        return 0
    return i + 1 if i % 2 == 1 else i - 1


def params():
    return pltpu.CompilerParams(vmem_limit_bytes=VMEM_LIMIT)


def cost(flops, moved):
    return pl.CostEstimate(flops=flops, bytes_accessed=moved, transcendentals=0)


def whole():
    return pl.BlockSpec(memory_space=pltpu.VMEM)


def anywhere():
    return pl.BlockSpec(memory_space=pl.ANY)


def origin_terms(place, velocity):
    px = place[0:1] * float(WX)
    py = place[1:2] * float(WY)
    pz = place[2:3] * float(NZ)
    return px, py, pz


def prepare_kernel(place, velocity, pop, up, down, sem):
    copies = []
    for k in range(5):
        rows = pl.ds(STATE_ROWS + k * WY, WY)
        copies.append(pltpu.make_async_copy(pop.at[X_UP[k], WX - 1], up.at[rows, :], sem.at[0]))
        copies.append(pltpu.make_async_copy(pop.at[X_DOWN[k], 0], down.at[rows, :], sem.at[0]))
    for copy in copies:
        copy.start()
    px, py, pz = origin_terms(place, velocity)
    wx, wy, wz = velocity[3:4], velocity[4:5], velocity[5:6]
    scale = 1.0 / LEVER_SCALE
    values = [
        velocity[0:1] - (wy * pz - wz * py) * scale,
        velocity[1:2] - (wz * px - wx * pz) * scale,
        velocity[2:3] - (wx * py - wy * px) * scale,
        wx,
        wy,
        wz,
    ]
    for c in range(6):
        for b in range(GROUPS):
            row = values[c][:, b * 128 : (b + 1) * 128]
            up[c * GROUPS + b : c * GROUPS + b + 1, :] = row
            down[c * GROUPS + b : c * GROUPS + b + 1, :] = row
    for copy in copies:
        copy.wait()


def prepare(place, velocity, populations):
    shape = jax.ShapeDtypeStruct((STATE_ROWS + FACE, 128), jnp.float32)
    return pl.pallas_call(
        prepare_kernel,
        out_shape=(shape, shape),
        in_specs=[whole(), whole(), anywhere()],
        out_specs=(whole(), whole()),
        scratch_shapes=[pltpu.SemaphoreType.DMA((1,))],
        compiler_params=params(),
        cost_estimate=cost(100_000, 600_000),
        name="prepare",
    )(place, velocity, populations)


def column_hot(cell):
    low = jnp.bitwise_and(jnp.right_shift(cell, 7), 511)
    rows = lax.broadcasted_iota(jnp.int32, (512, cell.shape[1]), 0)
    return jnp.where(rows == low, 1.0, 0.0).astype(jnp.bfloat16)


def depth_mask(cell):
    depth = jnp.bitwise_or(
        jnp.left_shift(jnp.right_shift(cell, 16), 7), jnp.bitwise_and(cell, 127)
    )
    rows = lax.broadcasted_iota(jnp.int32, (256, cell.shape[1]), 0)
    return rows == depth


NT = (((1,), (1,)), ((), ()))
NN = (((1,), (0,)), ((), ()))


def product(a, b, dims):
    return lax.dot_general(a, b, dims, preferred_element_type=jnp.float32)


def pick_kernel(cell, heading, floe, pop_hbm, dense, picked, up, down, pop, chosen, sem):
    load = pltpu.make_async_copy(pop_hbm, pop, sem.at[0])
    load.start()
    chosen[...] = jnp.zeros_like(chosen)

    def scatter(step, carry):
        at = pl.ds(pl.multiple_of(step * CHUNK, CHUNK), CHUNK)
        own = cell[:, at]
        value = jnp.where(floe[:, at] >= 0, heading[:, at], 0).astype(jnp.float32)
        hot = column_hot(own)
        payload = jnp.where(depth_mask(own), value, 0.0).astype(jnp.bfloat16)
        chosen[...] += product(hot, payload, NT)
        return carry

    lax.fori_loop(0, cell.shape[1] // CHUNK, scatter, 0)
    dense[0:512] = chosen[:, 0:128]
    dense[512:1024] = chosen[:, 128:256]
    load.wait()

    def select(step, carry):
        rows = pl.ds(pl.multiple_of(step * 32, 32), 32)
        for half in range(2):
            where = chosen[rows, half * 128 : (half + 1) * 128]
            source = pl.ds(pl.multiple_of(step * 32, 32) + half * 512, 32)
            value = jnp.zeros((32, 128), jnp.float32)
            for i in range(1, 19):
                value = jnp.where(where == float(i), pop[i, source, :], value)
            chosen[rows, half * 128 : (half + 1) * 128] = value
        return carry

    lax.fori_loop(0, 16, select, 0)
    turned = jnp.transpose(chosen[...])
    high = turned.astype(jnp.bfloat16)
    picked[0:256] = high
    picked[256:512] = (turned - high.astype(jnp.float32)).astype(jnp.bfloat16)
    for k in range(5):
        up[k * WX : (k + 1) * WX, :] = pop[Y_UP[k], pl.ds(WY - 1, WX, stride=WY), :]
        down[k * WX : (k + 1) * WX, :] = pop[Y_DOWN[k], pl.ds(0, WX, stride=WY), :]


def pick(cell, heading, floe, columns):
    face = jax.ShapeDtypeStruct((FACE, 128), jnp.float32)
    return pl.pallas_call(
        pick_kernel,
        out_shape=(
            jax.ShapeDtypeStruct((COLUMNS, NZ), jnp.float32),
            jax.ShapeDtypeStruct((512, 512), jnp.bfloat16),
            face,
            face,
        ),
        in_specs=[whole(), whole(), whole(), anywhere()],
        out_specs=(whole(),) * 4,
        scratch_shapes=[
            pltpu.VMEM(columns.shape, jnp.float32),
            pltpu.VMEM((512, 256), jnp.float32),
            pltpu.SemaphoreType.DMA((1,)),
        ],
        compiler_params=params(),
        cost_estimate=cost(2_200_000_000, 12_000_000),
        name="pick",
    )(cell, heading, floe, columns)


def gather_kernel(cell, picked, out):
    def step(t, carry):
        at = pl.ds(pl.multiple_of(t * CHUNK, CHUNK), CHUNK)
        own = cell[:, at]
        values = product(picked[...], column_hot(own), NN)
        values = values[0:256] + values[256:512]
        out[:, at] = jnp.sum(jnp.where(depth_mask(own), values, 0.0), axis=0, keepdims=True)
        return carry

    lax.fori_loop(0, cell.shape[1] // CHUNK, step, 0)


def gather(cell, picked):
    return pl.pallas_call(
        gather_kernel,
        out_shape=jax.ShapeDtypeStruct(cell.shape, jnp.float32),
        in_specs=[whole(), whole()],
        out_specs=whole(),
        compiler_params=params(),
        cost_estimate=cost(4_300_000_000, 1_000_000),
        name="gather",
    )(cell, picked)


def bits(table, heading):
    word = 0
    for i in table:
        word |= 1 << i
    return jnp.bitwise_and(jnp.right_shift(jnp.full_like(heading, word), heading), 1)


def component(axis, heading):
    plus = [i for i in range(19) if DIRECTIONS[i][axis] == 1]
    minus = [i for i in range(19) if DIRECTIONS[i][axis] == -1]
    return (bits(plus, heading) - bits(minus, heading)).astype(jnp.float32)


def floe_kernel(
    sizes, place, cell, heading, floe, here, mine, low, high, left, right,
    taken, loads_left, loads_mid, loads_right, table, spread, payload, total,
):
    size_along, size_across = sizes
    a = place[0]
    b = place[1]
    links = cell.shape[1]
    for ra in range(3):
        for rb in range(3):
            if rb == 0:
                state = left[ra * STATE_ROWS : (ra + 1) * STATE_ROWS]
            elif rb == 2:
                state = right[ra * STATE_ROWS : (ra + 1) * STATE_ROWS]
            else:
                state = (low, mine, high)[ra][0:STATE_ROWS]
            region = ra * 3 + rb
            lanes = slice(region * 128, (region + 1) * 128)
            first = state.astype(jnp.bfloat16)
            table[0:STATE_ROWS, lanes] = first
            table[STATE_ROWS : 2 * STATE_ROWS, lanes] = (
                state - first.astype(jnp.float32)
            ).astype(jnp.bfloat16)
    total[...] = jnp.zeros_like(total)
    payload[...] = jnp.zeros_like(payload)

    def step(t, carry):
        at = pl.ds(pl.multiple_of(t * CHUNK, CHUNK), CHUNK)
        k = cell[:, at]
        d = heading[:, at]
        g = floe[:, at]
        active = g >= 0
        owner = jnp.right_shift(g, 11)
        ra = jnp.bitwise_and(owner // size_across - a + 1, size_along - 1)
        rb = jnp.bitwise_and(jnp.bitwise_and(owner, size_across - 1) - b + 1, size_across - 1)
        member = jnp.bitwise_and(g, MEMBERS - 1)
        group = jnp.where(active, jnp.right_shift(member, 7), -1)
        entry = (ra * 3 + rb) * 128 + jnp.bitwise_and(member, 127)
        rows = lax.broadcasted_iota(jnp.int32, (9 * 128, CHUNK), 0)
        pick_floe = jnp.where(rows == entry, 1.0, 0.0).astype(jnp.bfloat16)
        groups = lax.broadcasted_iota(jnp.int32, (GROUPS, CHUNK), 0)
        mask = jnp.where(groups == group, 1.0, 0.0)

        cx = component(0, d)
        cy = component(1, d)
        cz = component(2, d)
        weight = jnp.where(d <= 6, WEIGHTS[1], WEIGHTS[7])
        lx = jnp.right_shift(k, 12)
        ly = jnp.bitwise_and(jnp.right_shift(k, 7), 31)
        lz = jnp.bitwise_and(k, 127)
        rx = ((1 - ra) * WX + lx).astype(jnp.float32) + 0.5 * cx
        ry = ((1 - rb) * WY + ly).astype(jnp.float32) + 0.5 * cy
        rz = lz.astype(jnp.float32) + 0.5 * cz
        scale = 1.0 / LEVER_SCALE
        coefficients = [
            cx,
            cy,
            cz,
            (ry * cz - rz * cy) * scale,
            (rz * cx - rx * cz) * scale,
            (rx * cy - ry * cx) * scale,
        ]
        for c in range(6):
            spread[c * GROUPS : (c + 1) * GROUPS, :] = mask * coefficients[c]

        state = product(table[...], pick_floe, NN)
        state = state[0:STATE_ROWS] + state[STATE_ROWS : 2 * STATE_ROWS]
        weights = spread[...]
        speed = jnp.sum(state * weights, axis=0, keepdims=True)
        take = (6.0 * FLOW_SCALE) * weight * speed
        magnitude = 2.0 * here[:, at] - take
        taken[:, at] = take
        amount = weights * magnitude
        first = amount.astype(jnp.bfloat16)
        payload[0:STATE_ROWS, :] = first
        payload[128 : 128 + STATE_ROWS, :] = (amount - first.astype(jnp.float32)).astype(
            jnp.bfloat16
        )
        total[...] += product(pick_floe, payload[...], NT)
        return carry

    lax.fori_loop(0, links // CHUNK, step, 0)
    for ra in range(3):
        for rb in range(3):
            rows = slice((ra * 3 + rb) * 128, (ra * 3 + rb + 1) * 128)
            summed = total[rows, 0:128] + total[rows, 128:256]
            out = (loads_left, loads_mid, loads_right)[rb]
            out[ra * STATE_ROWS : (ra + 1) * STATE_ROWS] = jnp.transpose(summed)[0:STATE_ROWS]


def floes(sizes, place, cell, heading, floe, here, mine, low, high, left, right):
    loads = jax.ShapeDtypeStruct((3 * STATE_ROWS, 128), jnp.float32)
    return pl.pallas_call(
        functools.partial(floe_kernel, sizes),
        out_shape=(jax.ShapeDtypeStruct(cell.shape, jnp.float32), loads, loads, loads),
        in_specs=[pl.BlockSpec(memory_space=pltpu.SMEM)] + [whole()] * 9,
        out_specs=(whole(),) * 4,
        scratch_shapes=[
            pltpu.VMEM((2 * STATE_ROWS, 9 * 128), jnp.bfloat16),
            pltpu.VMEM((STATE_ROWS, CHUNK), jnp.float32),
            pltpu.VMEM((256, CHUNK), jnp.bfloat16),
            pltpu.VMEM((9 * 128, 256), jnp.float32),
        ],
        compiler_params=params(),
        cost_estimate=cost(8_000_000_000, 2_000_000),
        name="floes",
    )(place, cell, heading, floe, here, mine, low, high, left, right)


def spread_kernel(cell, taken, dense, total):
    total[...] = jnp.zeros_like(total)

    def step(t, carry):
        at = pl.ds(pl.multiple_of(t * CHUNK, CHUNK), CHUNK)
        own = cell[:, at]
        value = taken[:, at]
        first = value.astype(jnp.bfloat16).astype(jnp.float32)
        mask = depth_mask(own)
        payload = jnp.concatenate(
            [
                jnp.where(mask, first, 0.0).astype(jnp.bfloat16),
                jnp.where(mask, value - first, 0.0).astype(jnp.bfloat16),
            ],
            axis=0,
        )
        total[...] += product(column_hot(own), payload, NT)
        return carry

    lax.fori_loop(0, cell.shape[1] // CHUNK, step, 0)
    dense[0:512] = total[:, 0:128] + total[:, 256:384]
    dense[512:1024] = total[:, 128:256] + total[:, 384:512]


def spread_out(cell, taken):
    return pl.pallas_call(
        spread_kernel,
        out_shape=jax.ShapeDtypeStruct((COLUMNS, NZ), jnp.float32),
        in_specs=[whole(), whole()],
        out_specs=whole(),
        scratch_shapes=[pltpu.VMEM((512, 512), jnp.float32)],
        compiler_params=params(),
        cost_estimate=cost(4_300_000_000, 1_000_000),
        name="spread",
    )(cell, taken)


SLAB = 4
SLABS = WX // SLAB
TOP = 8


def collide_kernel(
    dense_dir, dense_take, low, high, left, right, pop_hbm, out_hbm, pop, out, load_sem, store_sem
):
    def loading(s):
        return pltpu.make_async_copy(
            pop_hbm.at[:, pl.ds(s * SLAB, SLAB)],
            pop.at[:, pl.ds(1 + s * SLAB, SLAB), pl.ds(TOP, WY), :],
            load_sem.at[s],
        )

    for s in range(SLABS):
        loading(s).start()
    for k in range(5):
        rows = slice(STATE_ROWS + k * WY, STATE_ROWS + (k + 1) * WY)
        pop[X_UP[k], 0, TOP : TOP + WY, :] = low[rows, :]
        pop[X_DOWN[k], WX + 1, TOP : TOP + WY, :] = high[rows, :]
    base = 3 * STATE_ROWS
    for k in range(5):
        for x in range(WX):
            row = base + k * WX + x
            pop[Y_UP[k], 1 + x, TOP - 1 : TOP, :] = left[row : row + 1, :]
            pop[Y_DOWN[k], 1 + x, TOP + WY : TOP + WY + 1, :] = right[row : row + 1, :]
    edge = base + FACE
    pop[7, 0, TOP - 1 : TOP, :] = left[edge : edge + 1, :]
    pop[10, WX + 1, TOP - 1 : TOP, :] = left[edge + 1 : edge + 2, :]
    pop[9, 0, TOP + WY : TOP + WY + 1, :] = right[edge : edge + 1, :]
    pop[8, WX + 1, TOP + WY : TOP + WY + 1, :] = right[edge + 1 : edge + 2, :]

    def storing(s, slot):
        return pltpu.make_async_copy(
            out.at[slot], out_hbm.at[:, pl.ds(s * SLAB, SLAB)], store_sem.at[slot]
        )

    lane = lax.broadcasted_iota(jnp.int32, (8, 128), 1)
    first_lane = lane == 0
    last_lane = lane == NZ - 1
    rest = 1.0 - RELAXATION

    def tile(x, j, slot, inner):
        row = pl.multiple_of(x * WY, WY) + j * 8
        where = dense_dir[pl.ds(row, 8), :]
        take = dense_take[pl.ds(row, 8), :]

        def plain(i):
            return pop[i, x + 1, TOP + j * 8 : TOP + j * 8 + 8, :]

        def bounded(i, back):
            step_x, step_y, step_z = DIRECTIONS[i]
            start = TOP + j * 8 - step_y
            value = pop[i, x + 1 - step_x, start : start + 8, :]
            if step_z == 1:
                value = jnp.where(first_lane, back, pltpu.roll(value, 1, 1))
            elif step_z == -1:
                value = jnp.where(last_lane, back, pltpu.roll(value, NZ - 1, 1))
            return jnp.where(where == float(opposite(i)), back - take, value)

        centre = plain(0)
        density = centre
        both = []
        apart = []
        for i in range(1, 19, 2):
            plus = bounded(i, plain(i + 1))
            minus = bounded(i + 1, plain(i))
            both.append((plus, minus))
            apart.append(plus - minus)
            density = density + (plus + minus)
        d1, d3, d5, d7, d9, d11, d13, d15, d17 = apart
        mx = (d3 + d7) + (d9 + d11) + d13
        my = (d5 + d7) + (d15 - d9) + d17
        mz = (d1 + d11) + (d15 - d13) - d17
        inverse = 1.0 / density
        ux = mx * inverse
        uy = my * inverse
        uz = mz * inverse
        scaled = density * RELAXATION
        flat = scaled * (1.0 - 1.5 * (ux * ux + uy * uy + uz * uz))
        linear = 3.0 * scaled
        square = 4.5 * scaled
        out[slot, 0, inner, j * 8 : j * 8 + 8, :] = rest * centre + WEIGHTS[0] * flat
        for n in range(9):
            i = 2 * n + 1
            step_x, step_y, step_z = DIRECTIONS[i]
            projection = None
            for step, u in ((step_x, ux), (step_y, uy), (step_z, uz)):
                if step == 0:
                    continue
                if projection is None:
                    projection = u
                else:
                    projection = projection + u if step == 1 else projection - u
            even = WEIGHTS[i] * (flat + square * (projection * projection))
            odd = WEIGHTS[i] * (linear * projection)
            plus, minus = both[n]
            out[slot, i, inner, j * 8 : j * 8 + 8, :] = rest * plus + (even + odd)
            out[slot, i + 1, inner, j * 8 : j * 8 + 8, :] = rest * minus + (even - odd)

    loading(0).wait()

    def slab(s, carry):
        slot = lax.rem(s, 2)

        @pl.when(s + 1 < SLABS)
        def _():
            loading(s + 1).wait()

        @pl.when(s >= 2)
        def _():
            storing(s - 2, slot).wait()

        def plane(inner, inside):
            for j in range(WY // 8):
                tile(s * SLAB + inner, j, slot, inner)
            return inside

        lax.fori_loop(0, SLAB, plane, 0)
        storing(s, slot).start()
        return carry

    lax.fori_loop(0, SLABS, slab, 0)
    storing(SLABS - 2, (SLABS - 2) % 2).wait()
    storing(SLABS - 1, (SLABS - 1) % 2).wait()


def collide(dense_dir, dense_take, low, high, left, right, populations):
    return pl.pallas_call(
        collide_kernel,
        out_shape=jax.ShapeDtypeStruct(populations.shape, jnp.float32),
        in_specs=[whole()] * 6 + [anywhere()],
        out_specs=anywhere(),
        scratch_shapes=[
            pltpu.VMEM((19, WX + 2, WY + 16, NZ), jnp.float32),
            pltpu.VMEM((2, 19, SLAB, WY, NZ), jnp.float32),
            pltpu.SemaphoreType.DMA((SLABS,)),
            pltpu.SemaphoreType.DMA((2,)),
        ],
        compiler_params=params(),
        cost_estimate=cost(40_000_000, 24_000_000),
        name="collide",
    )(dense_dir, dense_take, low, high, left, right, populations)


def motion_kernel(own, low, high, place, velocity, response, out):
    loads = own[...] + low[...] + high[...]
    px, py, pz = origin_terms(place, velocity)
    scale = 1.0 / LEVER_SCALE
    for b in range(GROUPS):
        lanes = slice(b * 128, (b + 1) * 128)

        def load(c):
            return loads[c * GROUPS + b : c * GROUPS + b + 1, :]

        fx, fy, fz = load(0), load(1), load(2)
        qx, qy, qz = px[:, lanes], py[:, lanes], pz[:, lanes]
        torques = [
            load(3) - (qy * fz - qz * fy) * scale,
            load(4) - (qz * fx - qx * fz) * scale,
            load(5) - (qx * fy - qy * fx) * scale,
        ]
        for c, value in enumerate((fx, fy, fz)):
            out[c : c + 1, lanes] = velocity[c : c + 1, lanes] + response[0:1, lanes] * value
        for c, value in enumerate(torques):
            out[c + 3 : c + 4, lanes] = (
                velocity[c + 3 : c + 4, lanes] + response[1:2, lanes] * value
            )


def motion(own, low, high, place, velocity, response):
    return pl.pallas_call(
        motion_kernel,
        out_shape=jax.ShapeDtypeStruct(velocity.shape, jnp.float32),
        in_specs=[whole()] * 6,
        out_specs=whole(),
        compiler_params=params(),
        cost_estimate=cost(200_000, 300_000),
        name="motion",
    )(own, low, high, place, velocity, response)


def shifted(value, axis, step):
    count = lax.axis_size(axis)
    return lax.ppermute(value, axis, [(i, (i + step) % count) for i in range(count)])


def body(populations, link_cell, link_dir, link_floe, floe_place, floe_velocity, floe_response):
    sizes = (lax.axis_size("along"), lax.axis_size("across"))
    where = jnp.stack([lax.axis_index("along"), lax.axis_index("across")]).astype(jnp.int32)
    links = link_cell.shape[-1]
    cell = link_cell.reshape(1, links)
    heading = link_dir.reshape(1, links)
    floe = link_floe.reshape(1, links)
    columns = populations.reshape(19, COLUMNS, NZ)

    up, down = prepare(floe_place, floe_velocity, populations)
    low = shifted(up, "along", 1)
    high = shifted(down, "along", -1)
    dense_dir, picked, face_up, face_down = pick(cell, heading, floe, columns)

    def rows(block, k, y):
        at = STATE_ROWS + k * WY + y
        return block[at : at + 1]

    states = [low[:STATE_ROWS], up[:STATE_ROWS], high[:STATE_ROWS]]
    filler = jnp.zeros((EDGE_ROWS - 2, 128), jnp.float32)
    to_up = jnp.concatenate(
        states + [face_up, rows(low, X_UP.index(7), WY - 1), rows(high, X_DOWN.index(10), WY - 1)]
        + [filler]
    )
    to_down = jnp.concatenate(
        states + [face_down, rows(low, X_UP.index(9), 0), rows(high, X_DOWN.index(8), 0), filler]
    )
    left = shifted(to_up, "across", 1)
    right = shifted(to_down, "across", -1)
    here = gather(cell, picked)
    taken, loads_left, loads_mid, loads_right = floes(
        sizes, where, cell, heading, floe, here, up, low, high, left, right
    )
    from_right = shifted(loads_left, "across", -1)
    from_left = shifted(loads_right, "across", 1)
    dense_take = spread_out(cell, taken)
    three = loads_mid + from_left + from_right
    from_high = shifted(three[:STATE_ROWS], "along", -1)
    from_low = shifted(three[2 * STATE_ROWS :], "along", 1)
    relaxed = collide(dense_dir, dense_take, low, high, left, right, populations)
    moved = motion(
        three[STATE_ROWS : 2 * STATE_ROWS],
        from_low,
        from_high,
        floe_place,
        floe_velocity,
        floe_response,
    )
    return relaxed, moved


def solution(mesh):
    placed = (
        P(None, "along", "across", None),
        P("along", "across", None),
        P("along", "across", None),
        P("along", "across", None),
        P(None, ("along", "across")),
        P(None, ("along", "across")),
        P(None, ("along", "across")),
    )
    return jax.shard_map(
        body,
        mesh=mesh,
        in_specs=placed,
        out_specs=(P(None, "along", "across", None), P(None, ("along", "across"))),
        check_vma=False,
    )
```

```python
import functools

import jax
import jax.numpy as jnp
from jax import lax
from jax.experimental import pallas as pl
from jax.experimental.pallas import tpu as pltpu
from jax.sharding import PartitionSpec as P

DIRECTIONS = [
    (0, 0, 0),
    (0, 0, 1),
    (0, 0, -1),
    (1, 0, 0),
    (-1, 0, 0),
    (0, 1, 0),
    (0, -1, 0),
    (1, 1, 0),
    (-1, -1, 0),
    (1, -1, 0),
    (-1, 1, 0),
    (1, 0, 1),
    (-1, 0, -1),
    (1, 0, -1),
    (-1, 0, 1),
    (0, 1, 1),
    (0, -1, -1),
    (0, 1, -1),
    (0, -1, 1),
]
WEIGHTS = [1.0 / 3.0] + [1.0 / 18.0] * 6 + [1.0 / 36.0] * 12
RELAXATION = 1.0 / 0.6
FLOW_SCALE = 0.02
LEVER_SCALE = 64.0

WX = 32
WY = 32
NZ = 128
COLUMNS = WX * WY
MEMBERS = 2048
GROUPS = MEMBERS // 128
STATE_ROWS = 6 * GROUPS
FACE = 5 * WX
EDGE_ROWS = 8
WINDOW = 160
PADDED_COLUMNS = COLUMNS + WINDOW
CHUNK = 1024

X_UP = [i for i in range(19) if DIRECTIONS[i][0] == 1]
X_DOWN = [i for i in range(19) if DIRECTIONS[i][0] == -1]
Y_UP = [i for i in range(19) if DIRECTIONS[i][1] == 1]
Y_DOWN = [i for i in range(19) if DIRECTIONS[i][1] == -1]

VMEM_LIMIT = 58 * 1024 * 1024


def opposite(i):
    if i == 0:
        return 0
    return i + 1 if i % 2 == 1 else i - 1


def params():
    return pltpu.CompilerParams(vmem_limit_bytes=VMEM_LIMIT)


def cost(flops, moved):
    return pl.CostEstimate(flops=flops, bytes_accessed=moved, transcendentals=0)


def whole():
    return pl.BlockSpec(memory_space=pltpu.VMEM)


def anywhere():
    return pl.BlockSpec(memory_space=pl.ANY)


def origin_terms(place, velocity):
    px = place[0:1] * float(WX)
    py = place[1:2] * float(WY)
    pz = place[2:3] * float(NZ)
    return px, py, pz


def prepare_kernel(
    place, velocity, pop, up, down, face_up, face_down, ends_up, ends_down, sem, face_sem
):
    faces = []
    for k in range(5):
        faces.append(
            pltpu.make_async_copy(
                pop.at[Y_UP[k], :, pl.ds(WY - 8, 8), :], ends_up.at[k], face_sem.at[0]
            )
        )
        faces.append(
            pltpu.make_async_copy(pop.at[Y_DOWN[k], :, pl.ds(0, 8), :], ends_down.at[k], face_sem.at[0])
        )
    copies = []
    for k in range(5):
        rows = pl.ds(STATE_ROWS + k * WY, WY)
        copies.append(pltpu.make_async_copy(pop.at[X_UP[k], WX - 1], up.at[rows, :], sem.at[0]))
        copies.append(pltpu.make_async_copy(pop.at[X_DOWN[k], 0], down.at[rows, :], sem.at[0]))
    for copy in faces + copies:
        copy.start()
    px, py, pz = origin_terms(place, velocity)
    wx, wy, wz = velocity[3:4], velocity[4:5], velocity[5:6]
    scale = 1.0 / LEVER_SCALE
    values = [
        velocity[0:1] - (wy * pz - wz * py) * scale,
        velocity[1:2] - (wz * px - wx * pz) * scale,
        velocity[2:3] - (wx * py - wy * px) * scale,
        wx,
        wy,
        wz,
    ]
    for c in range(6):
        for b in range(GROUPS):
            row = values[c][:, b * 128 : (b + 1) * 128]
            up[c * GROUPS + b : c * GROUPS + b + 1, :] = row
            down[c * GROUPS + b : c * GROUPS + b + 1, :] = row
    for copy in faces:
        copy.wait()
    for k in range(5):
        face_up[k * WX : (k + 1) * WX, :] = ends_up[k, :, 7, :]
        face_down[k * WX : (k + 1) * WX, :] = ends_down[k, :, 0, :]
    for copy in copies:
        copy.wait()


def prepare(place, velocity, populations):
    shape = jax.ShapeDtypeStruct((STATE_ROWS + FACE, 128), jnp.float32)
    face = jax.ShapeDtypeStruct((FACE, 128), jnp.float32)
    return pl.pallas_call(
        prepare_kernel,
        out_shape=(shape, shape, face, face),
        in_specs=[whole(), whole(), anywhere()],
        out_specs=(whole(),) * 4,
        scratch_shapes=[
            pltpu.VMEM((5, WX, 8, NZ), jnp.float32),
            pltpu.VMEM((5, WX, 8, NZ), jnp.float32),
            pltpu.SemaphoreType.DMA((1,)),
            pltpu.SemaphoreType.DMA((1,)),
        ],
        compiler_params=params(),
        cost_estimate=cost(100_000, 2_600_000),
        name="prepare",
    )(place, velocity, populations)


NT = (((1,), (1,)), ((), ()))
NN = (((1,), (0,)), ((), ()))


def product(a, b, dims):
    return lax.dot_general(a, b, dims, preferred_element_type=jnp.float32)


def column_hot(cell, start):
    rows = lax.broadcasted_iota(jnp.int32, (WINDOW, cell.shape[1]), 0)
    return jnp.where(rows == jnp.right_shift(cell, 7) - start, 1.0, 0.0).astype(jnp.bfloat16)


def depth_mask(cell):
    rows = lax.broadcasted_iota(jnp.int32, (NZ, cell.shape[1]), 0)
    return rows == jnp.bitwise_and(cell, NZ - 1)


def sorted_chunks(keys, values):
    lane = lax.broadcasted_iota(jnp.int32, (8, 128), 1)
    sublane = lax.broadcasted_iota(jnp.int32, (8, 128), 0)

    def bit(position):
        if position < 6:
            return jnp.bitwise_and(jnp.right_shift(sublane, position - 3), 1)
        return jnp.bitwise_and(jnp.right_shift(lane, position - 6), 1)

    def partner(x, position):
        axis = 0 if position < 6 else 1
        extent = x.shape[axis]
        distance = 1 << (position - (3 if position < 6 else 6))
        if 2 * distance == extent:
            return pltpu.roll(x, distance, axis)
        return jnp.where(
            bit(position) == 0,
            pltpu.roll(x, extent - distance, axis),
            pltpu.roll(x, distance, axis),
        )

    for merge in range(1, 14):
        for position in range(merge - 1, -1, -1):
            if merge == 13 and position < 10:
                continue
            if position < 3:
                for v in range(8):
                    u = v | (1 << position)
                    if u == v:
                        continue
                    below = keys[u] < keys[v]
                    if merge < 3:
                        if (v >> merge) & 1:
                            below = keys[u] > keys[v]
                    elif merge < 13:
                        below = jnp.logical_xor(below, bit(merge) == 1)
                    keys[v], keys[u] = (
                        jnp.where(below, keys[u], keys[v]),
                        jnp.where(below, keys[v], keys[u]),
                    )
                    values[v], values[u] = (
                        jnp.where(below, values[u], values[v]),
                        jnp.where(below, values[v], values[u]),
                    )
                continue
            if merge < 13:
                least = bit(position) == bit(merge)
            else:
                least = bit(position) == 0
            for v in range(8):
                other = partner(keys[v], position)
                carried = partner(values[v], position)
                stay = jnp.logical_xor(other < keys[v], least)
                keys[v] = jnp.where(stay, keys[v], other)
                values[v] = jnp.where(stay, values[v], carried)
    return keys, values


def pick_kernel(sizes, place, cell, heading, floe, cells, words, work, dense, turned):
    size_along, size_across = sizes
    a = place[0]
    b = place[1]
    keys = []
    values = []
    for v in range(8):
        rows = slice(v * 8, (v + 1) * 8)
        g = floe[rows, :]
        owner = jnp.right_shift(g, 11)
        ra = jnp.bitwise_and(owner // size_across - a + 1, size_along - 1)
        rb = jnp.bitwise_and(jnp.bitwise_and(owner, size_across - 1) - b + 1, size_across - 1)
        entry = (ra * 3 + rb) * MEMBERS + jnp.bitwise_and(g, MEMBERS - 1)
        word = jnp.left_shift(heading[rows, :], 15) + entry
        keys.append(cell[rows, :])
        values.append(jnp.where(g >= 0, word, 9 * MEMBERS))
    keys, values = sorted_chunks(keys, values)
    turned[...] = jnp.transpose(jnp.concatenate(keys + values, axis=0))
    even = turned[pl.ds(0, 64, stride=2), :]
    odd = turned[pl.ds(1, 64, stride=2), :]
    left = lax.broadcasted_iota(jnp.int32, (64, 128), 1) < 64
    key = jnp.where(left, even, pltpu.roll(odd, 64, 1))
    value = jnp.where(left, pltpu.roll(even, 64, 1), odd)
    for r in range(64):
        cells[:, r * 128 : (r + 1) * 128] = key[r : r + 1, :]
        words[:, r * 128 : (r + 1) * 128] = value[r : r + 1, :]
    column = jnp.right_shift(key, 7)
    count = jnp.int32(8)
    for c in range(8):
        part = column[c * 8 : (c + 1) * 8, :]
        first = jnp.left_shift(jnp.right_shift(jnp.min(part), 3), 3)
        last = jnp.max(part)
        windows = (last - first) // WINDOW + 1
        work[0, c] = c
        work[1, c] = first

        def enter(w, n, c=c, first=first):
            work[0, n] = c
            work[1, n] = first + w * WINDOW
            return n + 1

        count = lax.fori_loop(1, windows, enter, count)
    work[2, 0] = count
    dense[...] = jnp.zeros_like(dense)

    def scatter(at, start):
        own = cells[:, at]
        kind = jnp.right_shift(words[:, at], 15).astype(jnp.float32)
        payload = jnp.where(depth_mask(own), kind, 0.0).astype(jnp.bfloat16)
        return product(column_hot(own, start), payload, NT)

    over_windows(work, scatter, window_adder(dense))


def window_adder(dense):
    def add(at, start, value):
        dense[pl.ds(start, WINDOW), :] += value

    return add


def over_windows(work, compute, apply):
    for group in range(0, 8, 4):
        results = []
        for c in range(group, group + 4):
            at = slice(c * 1024, (c + 1) * 1024)
            start = pl.multiple_of(work[1, c], 8)
            results.append((at, start, compute(at, start)))
        for result in results:
            apply(*result)

    def step(n, carry):
        at = pl.ds(pl.multiple_of(work[0, n] * 1024, 1024), 1024)
        start = pl.multiple_of(work[1, n], 8)
        apply(at, start, compute(at, start))
        return carry

    lax.fori_loop(8, work[2, 0], step, 0)


def smem():
    return pl.BlockSpec(memory_space=pltpu.SMEM)


def pick(sizes, place, cell, heading, floe):
    links = cell.shape[0] * cell.shape[1]
    row = jax.ShapeDtypeStruct((1, links), jnp.int32)
    return pl.pallas_call(
        functools.partial(pick_kernel, sizes),
        out_shape=(
            row,
            row,
            jax.ShapeDtypeStruct((3, 32), jnp.int32),
            jax.ShapeDtypeStruct((PADDED_COLUMNS, NZ), jnp.float32),
        ),
        in_specs=[smem(), whole(), whole(), whole()],
        out_specs=(whole(), whole(), smem(), whole()),
        scratch_shapes=[pltpu.VMEM((128, 128), jnp.int32)],
        compiler_params=params(),
        cost_estimate=cost(7_000_000_000, 1_000_000),
        name="pick",
    )(place, cell, heading, floe)


def gather_kernel(work, cell, dense, pop_hbm, out, pop, chosen, sem):
    def loading(s):
        return pltpu.make_async_copy(
            pop_hbm.at[:, pl.ds(s * 128, 128)], pop.at[:, pl.ds(s * 128, 128)], sem.at[s]
        )

    for s in range(8):
        loading(s).start()
    chosen[COLUMNS:] = jnp.zeros((PADDED_COLUMNS - COLUMNS, NZ), jnp.float32)
    out[...] = jnp.zeros_like(out)

    def select(s, carry):
        loading(s).wait()
        for part in range(4):
            rows = pl.ds(pl.multiple_of(s * 128, 128) + part * 32, 32)
            where = dense[rows, :]
            value = jnp.zeros((32, 128), jnp.float32)
            for i in range(1, 19):
                value = jnp.where(where == float(i), pop[i, rows, :], value)
            chosen[rows, :] = value
        return carry

    lax.fori_loop(0, 8, select, 0)

    def read(at, start):
        own = cell[:, at]
        turned = jnp.transpose(chosen[pl.ds(start, WINDOW), :])
        high = turned.astype(jnp.bfloat16)
        low = (turned - high.astype(jnp.float32)).astype(jnp.bfloat16)
        values = product(jnp.concatenate([high, low], axis=0), column_hot(own, start), NN)
        values = values[0:NZ] + values[NZ : 2 * NZ]
        return jnp.sum(jnp.where(depth_mask(own), values, 0.0), axis=0, keepdims=True)

    def add(at, start, value):
        out[:, at] += value

    over_windows(work, read, add)


def gather(work, cell, dense, columns):
    return pl.pallas_call(
        gather_kernel,
        out_shape=jax.ShapeDtypeStruct(cell.shape, jnp.float32),
        in_specs=[smem(), whole(), whole(), anywhere()],
        out_specs=whole(),
        scratch_shapes=[
            pltpu.VMEM(columns.shape, jnp.float32),
            pltpu.VMEM((PADDED_COLUMNS, NZ), jnp.float32),
            pltpu.SemaphoreType.DMA((8,)),
        ],
        compiler_params=params(),
        cost_estimate=cost(6_000_000_000, 12_000_000),
        name="gather",
    )(work, cell, dense, columns)


def bits(table, heading):
    word = 0
    for i in table:
        word |= 1 << i
    return jnp.bitwise_and(jnp.right_shift(jnp.full_like(heading, word), heading), 1)


def component(axis, heading):
    plus = [i for i in range(19) if DIRECTIONS[i][axis] == 1]
    minus = [i for i in range(19) if DIRECTIONS[i][axis] == -1]
    return (bits(plus, heading) - bits(minus, heading)).astype(jnp.float32)


def floe_kernel(
    cell, words, here, mine, low, high, left, right,
    taken, loads_left, loads_mid, loads_right, table, hot, spread, payload, total,
):
    links = cell.shape[1]
    for ra in range(3):
        for rb in range(3):
            if rb == 0:
                state = left[ra * STATE_ROWS : (ra + 1) * STATE_ROWS]
            elif rb == 2:
                state = right[ra * STATE_ROWS : (ra + 1) * STATE_ROWS]
            else:
                state = (low, mine, high)[ra][0:STATE_ROWS]
            region = ra * 3 + rb
            lanes = slice(region * 128, (region + 1) * 128)
            first = state.astype(jnp.bfloat16)
            table[0:STATE_ROWS, lanes] = first
            table[STATE_ROWS : 2 * STATE_ROWS, lanes] = (
                state - first.astype(jnp.float32)
            ).astype(jnp.bfloat16)
    payload[...] = jnp.zeros_like(payload)

    def first_half(t):
        slot = t % 2
        at = slice(t * CHUNK, (t + 1) * CHUNK)
        k = cell[:, at]
        word = words[:, at]
        d = jnp.right_shift(word, 15)
        place = jnp.bitwise_and(word, 32767)
        region = jnp.right_shift(place, 11)
        ra = jnp.right_shift(region * 11, 5)
        rb = region - 3 * ra
        group = jnp.bitwise_and(jnp.right_shift(place, 7), GROUPS - 1)
        entry = region * 128 + jnp.bitwise_and(place, 127)
        rows = lax.broadcasted_iota(jnp.int32, (9 * 128, CHUNK), 0)
        pick_floe = jnp.where(rows == entry, 1.0, 0.0).astype(jnp.bfloat16)
        groups = lax.broadcasted_iota(jnp.int32, (GROUPS, CHUNK), 0)
        mask = jnp.where(groups == group, 1.0, 0.0)

        cx = component(0, d)
        cy = component(1, d)
        cz = component(2, d)
        weight = jnp.where(d <= 6, WEIGHTS[1], WEIGHTS[7])
        lx = jnp.right_shift(k, 12)
        ly = jnp.bitwise_and(jnp.right_shift(k, 7), 31)
        lz = jnp.bitwise_and(k, 127)
        rx = ((1 - ra) * WX + lx).astype(jnp.float32) + 0.5 * cx
        ry = ((1 - rb) * WY + ly).astype(jnp.float32) + 0.5 * cy
        rz = lz.astype(jnp.float32) + 0.5 * cz
        scale = 1.0 / LEVER_SCALE
        coefficients = [
            cx,
            cy,
            cz,
            (ry * cz - rz * cy) * scale,
            (rz * cx - rx * cz) * scale,
            (rx * cy - ry * cx) * scale,
        ]
        for c in range(6):
            spread[slot, c * GROUPS : (c + 1) * GROUPS, :] = mask * coefficients[c]
        hot[slot] = pick_floe

        state = product(table[...], pick_floe, NN)
        state = state[0:STATE_ROWS] + state[STATE_ROWS : 2 * STATE_ROWS]
        weights = spread[slot]
        speed = jnp.sum(state * weights, axis=0, keepdims=True)
        take = (6.0 * FLOW_SCALE) * weight * speed
        magnitude = 2.0 * here[:, at] - take
        taken[:, at] = take
        amount = weights * magnitude
        first = amount.astype(jnp.bfloat16)
        payload[slot, 0:STATE_ROWS, :] = first
        payload[slot, 128 : 128 + STATE_ROWS, :] = (amount - first.astype(jnp.float32)).astype(
            jnp.bfloat16
        )

    def second_half(t):
        value = product(hot[t % 2], payload[t % 2], NT)
        if t == 0:
            total[...] = value
        else:
            total[...] += value

    steps = links // CHUNK
    first_half(0)
    for t in range(1, steps):
        first_half(t)
        second_half(t - 1)
    second_half(steps - 1)
    for ra in range(3):
        for rb in range(3):
            rows = slice((ra * 3 + rb) * 128, (ra * 3 + rb + 1) * 128)
            summed = total[rows, 0:128] + total[rows, 128:256]
            out = (loads_left, loads_mid, loads_right)[rb]
            out[ra * STATE_ROWS : (ra + 1) * STATE_ROWS] = jnp.transpose(summed)[0:STATE_ROWS]


def floes(cell, words, here, mine, low, high, left, right):
    loads = jax.ShapeDtypeStruct((3 * STATE_ROWS, 128), jnp.float32)
    return pl.pallas_call(
        floe_kernel,
        out_shape=(jax.ShapeDtypeStruct(cell.shape, jnp.float32), loads, loads, loads),
        in_specs=[whole()] * 8,
        out_specs=(whole(),) * 4,
        scratch_shapes=[
            pltpu.VMEM((2 * STATE_ROWS, 9 * 128), jnp.bfloat16),
            pltpu.VMEM((2, 9 * 128, CHUNK), jnp.bfloat16),
            pltpu.VMEM((2, STATE_ROWS, CHUNK), jnp.float32),
            pltpu.VMEM((2, 256, CHUNK), jnp.bfloat16),
            pltpu.VMEM((9 * 128, 256), jnp.float32),
        ],
        compiler_params=params(),
        cost_estimate=cost(8_000_000_000, 2_000_000),
        name="floes",
    )(cell, words, here, mine, low, high, left, right)


def spread_kernel(work, cell, taken, dense):
    dense[...] = jnp.zeros_like(dense)

    def scatter(at, start):
        own = cell[:, at]
        value = taken[:, at]
        first = value.astype(jnp.bfloat16).astype(jnp.float32)
        mask = depth_mask(own)
        payload = jnp.concatenate(
            [
                jnp.where(mask, first, 0.0).astype(jnp.bfloat16),
                jnp.where(mask, value - first, 0.0).astype(jnp.bfloat16),
            ],
            axis=0,
        )
        both = product(column_hot(own, start), payload, NT)
        return both[:, :NZ] + both[:, NZ:]

    over_windows(work, scatter, window_adder(dense))


def spread_out(work, cell, taken):
    return pl.pallas_call(
        spread_kernel,
        out_shape=jax.ShapeDtypeStruct((PADDED_COLUMNS, NZ), jnp.float32),
        in_specs=[smem(), whole(), whole()],
        out_specs=whole(),
        compiler_params=params(),
        cost_estimate=cost(3_000_000_000, 1_000_000),
        name="spread",
    )(work, cell, taken)


SLAB = 4
SLABS = WX // SLAB
TOP = 8


def collide_kernel(
    dense_dir, dense_take, low, high, left, right, pop_hbm, out_hbm, pop, out, load_sem, store_sem
):
    def loading(s):
        return pltpu.make_async_copy(
            pop_hbm.at[:, pl.ds(s * SLAB, SLAB)],
            pop.at[:, pl.ds(1 + s * SLAB, SLAB), pl.ds(TOP, WY), :],
            load_sem.at[s],
        )

    for s in range(SLABS):
        loading(s).start()
    for k in range(5):
        rows = slice(STATE_ROWS + k * WY, STATE_ROWS + (k + 1) * WY)
        pop[X_UP[k], 0, TOP : TOP + WY, :] = low[rows, :]
        pop[X_DOWN[k], WX + 1, TOP : TOP + WY, :] = high[rows, :]
    base = 3 * STATE_ROWS
    for k in range(5):
        for x in range(WX):
            row = base + k * WX + x
            pop[Y_UP[k], 1 + x, TOP - 1 : TOP, :] = left[row : row + 1, :]
            pop[Y_DOWN[k], 1 + x, TOP + WY : TOP + WY + 1, :] = right[row : row + 1, :]
    edge = base + FACE
    pop[7, 0, TOP - 1 : TOP, :] = left[edge : edge + 1, :]
    pop[10, WX + 1, TOP - 1 : TOP, :] = left[edge + 1 : edge + 2, :]
    pop[9, 0, TOP + WY : TOP + WY + 1, :] = right[edge : edge + 1, :]
    pop[8, WX + 1, TOP + WY : TOP + WY + 1, :] = right[edge + 1 : edge + 2, :]

    def storing(s, slot):
        return pltpu.make_async_copy(
            out.at[slot], out_hbm.at[:, pl.ds(s * SLAB, SLAB)], store_sem.at[slot]
        )

    lane = lax.broadcasted_iota(jnp.int32, (8, 128), 1)
    first_lane = lane == 0
    last_lane = lane == NZ - 1
    rest = 1.0 - RELAXATION

    def tile(x, j, slot, inner):
        row = pl.multiple_of(x * WY, WY) + j * 8
        where = dense_dir[pl.ds(row, 8), :]
        take = dense_take[pl.ds(row, 8), :]

        def plain(i):
            return pop[i, x + 1, TOP + j * 8 : TOP + j * 8 + 8, :]

        def bounded(i, back):
            step_x, step_y, step_z = DIRECTIONS[i]
            start = TOP + j * 8 - step_y
            value = pop[i, x + 1 - step_x, start : start + 8, :]
            if step_z == 1:
                value = jnp.where(first_lane, back, pltpu.roll(value, 1, 1))
            elif step_z == -1:
                value = jnp.where(last_lane, back, pltpu.roll(value, NZ - 1, 1))
            return jnp.where(where == float(opposite(i)), back - take, value)

        centre = plain(0)
        density = centre
        both = []
        apart = []
        for i in range(1, 19, 2):
            plus = bounded(i, plain(i + 1))
            minus = bounded(i + 1, plain(i))
            both.append((plus, minus))
            apart.append(plus - minus)
            density = density + (plus + minus)
        d1, d3, d5, d7, d9, d11, d13, d15, d17 = apart
        mx = (d3 + d7) + (d9 + d11) + d13
        my = (d5 + d7) + (d15 - d9) + d17
        mz = (d1 + d11) + (d15 - d13) - d17
        inverse = 1.0 / density
        ux = mx * inverse
        uy = my * inverse
        uz = mz * inverse
        scaled = density * RELAXATION
        flat = scaled * (1.0 - 1.5 * (ux * ux + uy * uy + uz * uz))
        linear = 3.0 * scaled
        square = 4.5 * scaled
        out[slot, 0, inner, j * 8 : j * 8 + 8, :] = rest * centre + WEIGHTS[0] * flat
        for n in range(9):
            i = 2 * n + 1
            step_x, step_y, step_z = DIRECTIONS[i]
            projection = None
            for step, u in ((step_x, ux), (step_y, uy), (step_z, uz)):
                if step == 0:
                    continue
                if projection is None:
                    projection = u
                else:
                    projection = projection + u if step == 1 else projection - u
            even = WEIGHTS[i] * (flat + square * (projection * projection))
            odd = WEIGHTS[i] * (linear * projection)
            plus, minus = both[n]
            out[slot, i, inner, j * 8 : j * 8 + 8, :] = rest * plus + (even + odd)
            out[slot, i + 1, inner, j * 8 : j * 8 + 8, :] = rest * minus + (even - odd)

    loading(0).wait()

    def slab(s, carry):
        slot = lax.rem(s, 2)

        @pl.when(s + 1 < SLABS)
        def _():
            loading(s + 1).wait()

        @pl.when(s >= 2)
        def _():
            storing(s - 2, slot).wait()

        def plane(inner, inside):
            for j in range(WY // 8):
                tile(s * SLAB + inner, j, slot, inner)
            return inside

        lax.fori_loop(0, SLAB, plane, 0)
        storing(s, slot).start()
        return carry

    lax.fori_loop(0, SLABS, slab, 0)
    storing(SLABS - 2, (SLABS - 2) % 2).wait()
    storing(SLABS - 1, (SLABS - 1) % 2).wait()


def collide(dense_dir, dense_take, low, high, left, right, populations):
    return pl.pallas_call(
        collide_kernel,
        out_shape=jax.ShapeDtypeStruct(populations.shape, jnp.float32),
        in_specs=[whole()] * 6 + [anywhere()],
        out_specs=anywhere(),
        scratch_shapes=[
            pltpu.VMEM((19, WX + 2, WY + 16, NZ), jnp.float32),
            pltpu.VMEM((2, 19, SLAB, WY, NZ), jnp.float32),
            pltpu.SemaphoreType.DMA((SLABS,)),
            pltpu.SemaphoreType.DMA((2,)),
        ],
        compiler_params=params(),
        cost_estimate=cost(40_000_000, 24_000_000),
        name="collide",
    )(dense_dir, dense_take, low, high, left, right, populations)


def motion_kernel(own, low, high, place, velocity, response, out):
    loads = own[...] + low[...] + high[...]
    px, py, pz = origin_terms(place, velocity)
    scale = 1.0 / LEVER_SCALE
    for b in range(GROUPS):
        lanes = slice(b * 128, (b + 1) * 128)

        def load(c):
            return loads[c * GROUPS + b : c * GROUPS + b + 1, :]

        fx, fy, fz = load(0), load(1), load(2)
        qx, qy, qz = px[:, lanes], py[:, lanes], pz[:, lanes]
        torques = [
            load(3) - (qy * fz - qz * fy) * scale,
            load(4) - (qz * fx - qx * fz) * scale,
            load(5) - (qx * fy - qy * fx) * scale,
        ]
        for c, value in enumerate((fx, fy, fz)):
            out[c : c + 1, lanes] = velocity[c : c + 1, lanes] + response[0:1, lanes] * value
        for c, value in enumerate(torques):
            out[c + 3 : c + 4, lanes] = (
                velocity[c + 3 : c + 4, lanes] + response[1:2, lanes] * value
            )


def motion(own, low, high, place, velocity, response):
    return pl.pallas_call(
        motion_kernel,
        out_shape=jax.ShapeDtypeStruct(velocity.shape, jnp.float32),
        in_specs=[whole()] * 6,
        out_specs=whole(),
        compiler_params=params(),
        cost_estimate=cost(200_000, 300_000),
        name="motion",
    )(own, low, high, place, velocity, response)


def shifted(value, axis, step):
    count = lax.axis_size(axis)
    return lax.ppermute(value, axis, [(i, (i + step) % count) for i in range(count)])


def body(populations, link_cell, link_dir, link_floe, floe_place, floe_velocity, floe_response):
    sizes = (lax.axis_size("along"), lax.axis_size("across"))
    where = jnp.stack([lax.axis_index("along"), lax.axis_index("across")]).astype(jnp.int32)
    links = link_cell.shape[-1]
    cell = link_cell.reshape(links // 128, 128)
    heading = link_dir.reshape(links // 128, 128)
    floe = link_floe.reshape(links // 128, 128)
    columns = populations.reshape(19, COLUMNS, NZ)

    up, down, face_up, face_down = prepare(floe_place, floe_velocity, populations)
    low = shifted(up, "along", 1)
    high = shifted(down, "along", -1)
    cells, words, work, dense_dir = pick(sizes, where, cell, heading, floe)

    def rows(block, k, y):
        at = STATE_ROWS + k * WY + y
        return block[at : at + 1]

    states = [low[:STATE_ROWS], up[:STATE_ROWS], high[:STATE_ROWS]]
    filler = jnp.zeros((EDGE_ROWS - 2, 128), jnp.float32)
    to_up = jnp.concatenate(
        states + [face_up, rows(low, X_UP.index(7), WY - 1), rows(high, X_DOWN.index(10), WY - 1)]
        + [filler]
    )
    to_down = jnp.concatenate(
        states + [face_down, rows(low, X_UP.index(9), 0), rows(high, X_DOWN.index(8), 0), filler]
    )
    left = shifted(to_up, "across", 1)
    right = shifted(to_down, "across", -1)
    here = gather(work, cells, dense_dir, columns)
    taken, loads_left, loads_mid, loads_right = floes(
        cells, words, here, up, low, high, left, right
    )
    from_right = shifted(loads_left, "across", -1)
    from_left = shifted(loads_right, "across", 1)
    dense_take = spread_out(work, cells, taken)
    three = loads_mid + from_left + from_right
    from_high = shifted(three[:STATE_ROWS], "along", -1)
    from_low = shifted(three[2 * STATE_ROWS :], "along", 1)
    relaxed = collide(dense_dir, dense_take, low, high, left, right, populations)
    moved = motion(
        three[STATE_ROWS : 2 * STATE_ROWS],
        from_low,
        from_high,
        floe_place,
        floe_velocity,
        floe_response,
    )
    return relaxed, moved


def solution(mesh):
    placed = (
        P(None, "along", "across", None),
        P("along", "across", None),
        P("along", "across", None),
        P("along", "across", None),
        P(None, ("along", "across")),
        P(None, ("along", "across")),
        P(None, ("along", "across")),
    )
    return jax.shard_map(
        body,
        mesh=mesh,
        in_specs=placed,
        out_specs=(P(None, "along", "across", None), P(None, ("along", "across"))),
        check_vma=False,
    )
```

```python
import functools

import jax
import jax.numpy as jnp
from jax import lax
from jax.experimental import pallas as pl
from jax.experimental.pallas import tpu as pltpu
from jax.sharding import PartitionSpec as P

DIRECTIONS = [
    (0, 0, 0),
    (0, 0, 1),
    (0, 0, -1),
    (1, 0, 0),
    (-1, 0, 0),
    (0, 1, 0),
    (0, -1, 0),
    (1, 1, 0),
    (-1, -1, 0),
    (1, -1, 0),
    (-1, 1, 0),
    (1, 0, 1),
    (-1, 0, -1),
    (1, 0, -1),
    (-1, 0, 1),
    (0, 1, 1),
    (0, -1, -1),
    (0, 1, -1),
    (0, -1, 1),
]
WEIGHTS = [1.0 / 3.0] + [1.0 / 18.0] * 6 + [1.0 / 36.0] * 12
RELAXATION = 1.0 / 0.6
FLOW_SCALE = 0.02
LEVER_SCALE = 64.0

WX = 32
WY = 32
NZ = 128
COLUMNS = WX * WY
MEMBERS = 2048
GROUPS = MEMBERS // 128
STATE_ROWS = 6 * GROUPS
FACE = 5 * WX
EDGE_ROWS = 8
WINDOW = 160
PADDED_COLUMNS = COLUMNS + WINDOW
CHUNK = 1024

X_UP = [i for i in range(19) if DIRECTIONS[i][0] == 1]
X_DOWN = [i for i in range(19) if DIRECTIONS[i][0] == -1]
Y_UP = [i for i in range(19) if DIRECTIONS[i][1] == 1]
Y_DOWN = [i for i in range(19) if DIRECTIONS[i][1] == -1]


def opposite(i):
    if i == 0:
        return 0
    return i + 1 if i % 2 == 1 else i - 1


def params(mebibytes):
    return pltpu.CompilerParams(vmem_limit_bytes=mebibytes * 1024 * 1024)


def cost(flops, moved):
    return pl.CostEstimate(flops=flops, bytes_accessed=moved, transcendentals=0)


def whole():
    return pl.BlockSpec(memory_space=pltpu.VMEM)


def anywhere():
    return pl.BlockSpec(memory_space=pl.ANY)


def origin_terms(place, velocity):
    px = place[0:1] * float(WX)
    py = place[1:2] * float(WY)
    pz = place[2:3] * float(NZ)
    return px, py, pz


def prepare_kernel(
    place, velocity, pop, up, down, sem
):
    copies = []
    for k in range(5):
        rows = pl.ds(STATE_ROWS + k * WY, WY)
        copies.append(pltpu.make_async_copy(pop.at[X_UP[k], WX - 1], up.at[rows, :], sem.at[0]))
        copies.append(pltpu.make_async_copy(pop.at[X_DOWN[k], 0], down.at[rows, :], sem.at[0]))
    for copy in copies:
        copy.start()
    px, py, pz = origin_terms(place, velocity)
    wx, wy, wz = velocity[3:4], velocity[4:5], velocity[5:6]
    scale = 1.0 / LEVER_SCALE
    values = [
        velocity[0:1] - (wy * pz - wz * py) * scale,
        velocity[1:2] - (wz * px - wx * pz) * scale,
        velocity[2:3] - (wx * py - wy * px) * scale,
        wx,
        wy,
        wz,
    ]
    for c in range(6):
        for b in range(GROUPS):
            row = values[c][:, b * 128 : (b + 1) * 128]
            up[c * GROUPS + b : c * GROUPS + b + 1, :] = row
            down[c * GROUPS + b : c * GROUPS + b + 1, :] = row
    for copy in copies:
        copy.wait()


def prepare(place, velocity, populations):
    shape = jax.ShapeDtypeStruct((STATE_ROWS + FACE, 128), jnp.float32)
    return pl.pallas_call(
        prepare_kernel,
        out_shape=(shape, shape),
        in_specs=[whole(), whole(), hbm()],
        out_specs=(whole(),) * 2,
        scratch_shapes=[pltpu.SemaphoreType.DMA((1,))],
        compiler_params=params(48),
        cost_estimate=cost(100_000, 2_600_000),
        name="prepare",
    )(place, velocity, populations)


NT = (((1,), (1,)), ((), ()))
NN = (((1,), (0,)), ((), ()))


def product(a, b, dims):
    return lax.dot_general(a, b, dims, preferred_element_type=jnp.float32)


def column_hot(cell, start):
    rows = lax.broadcasted_iota(jnp.int32, (WINDOW, cell.shape[1]), 0)
    return jnp.where(rows == jnp.right_shift(cell, 7) - start, 1.0, 0.0).astype(jnp.bfloat16)


def depth_mask(cell):
    rows = lax.broadcasted_iota(jnp.int32, (NZ, cell.shape[1]), 0)
    return rows == jnp.bitwise_and(cell, NZ - 1)


def sorted_chunks(keys, values):
    lane = lax.broadcasted_iota(jnp.int32, (8, 128), 1)
    sublane = lax.broadcasted_iota(jnp.int32, (8, 128), 0)

    def bit(position):
        if position < 6:
            return jnp.bitwise_and(jnp.right_shift(sublane, position - 3), 1)
        return jnp.bitwise_and(jnp.right_shift(lane, position - 6), 1)

    def partner(x, position):
        axis = 0 if position < 6 else 1
        extent = x.shape[axis]
        distance = 1 << (position - (3 if position < 6 else 6))
        if 2 * distance == extent:
            return pltpu.roll(x, distance, axis)
        return jnp.where(
            bit(position) == 0,
            pltpu.roll(x, extent - distance, axis),
            pltpu.roll(x, distance, axis),
        )

    for merge in range(1, 14):
        for position in range(merge - 1, -1, -1):
            if merge == 13 and position < 10:
                continue
            if position < 3:
                for v in range(8):
                    u = v | (1 << position)
                    if u == v:
                        continue
                    below = keys[u] < keys[v]
                    if merge < 3:
                        if (v >> merge) & 1:
                            below = keys[u] > keys[v]
                    elif merge < 13:
                        below = jnp.logical_xor(below, bit(merge) == 1)
                    keys[v], keys[u] = (
                        jnp.where(below, keys[u], keys[v]),
                        jnp.where(below, keys[v], keys[u]),
                    )
                    values[v], values[u] = (
                        jnp.where(below, values[u], values[v]),
                        jnp.where(below, values[v], values[u]),
                    )
                continue
            if merge < 13:
                least = bit(position) == bit(merge)
            else:
                least = bit(position) == 0
            for v in range(8):
                other = partner(keys[v], position)
                carried = partner(values[v], position)
                stay = jnp.logical_xor(other < keys[v], least)
                keys[v] = jnp.where(stay, keys[v], other)
                values[v] = jnp.where(stay, values[v], carried)
    return keys, values


def pick_kernel(
    sizes, cell, heading, floe, pop, cells, words, work, dense, chosen, face_up, face_down,
    turned, resident, sem,
):
    load = pltpu.make_async_copy(pop, resident, sem.at[0])
    load.start()
    size_along, size_across = sizes
    a = lax.axis_index("along")
    b = lax.axis_index("across")
    keys = []
    values = []
    for v in range(8):
        rows = slice(v * 8, (v + 1) * 8)
        g = floe[rows, :]
        owner = jnp.right_shift(g, 11)
        ra = jnp.bitwise_and(owner // size_across - a + 1, size_along - 1)
        rb = jnp.bitwise_and(jnp.bitwise_and(owner, size_across - 1) - b + 1, size_across - 1)
        entry = (ra * 3 + rb) * MEMBERS + jnp.bitwise_and(g, MEMBERS - 1)
        word = jnp.left_shift(heading[rows, :], 15) + entry
        keys.append(cell[rows, :])
        values.append(jnp.where(g >= 0, word, 9 * MEMBERS))
    keys, values = sorted_chunks(keys, values)
    turned[...] = jnp.transpose(jnp.concatenate(keys + values, axis=0))
    even = turned[pl.ds(0, 64, stride=2), :]
    odd = turned[pl.ds(1, 64, stride=2), :]
    left = lax.broadcasted_iota(jnp.int32, (64, 128), 1) < 64
    key = jnp.where(left, even, pltpu.roll(odd, 64, 1))
    value = jnp.where(left, pltpu.roll(even, 64, 1), odd)
    for r in range(64):
        cells[:, r * 128 : (r + 1) * 128] = key[r : r + 1, :]
        words[:, r * 128 : (r + 1) * 128] = value[r : r + 1, :]
    column = jnp.right_shift(key, 7)
    count = jnp.int32(8)
    for c in range(8):
        part = column[c * 8 : (c + 1) * 8, :]
        first = jnp.left_shift(jnp.right_shift(jnp.min(part), 3), 3)
        last = jnp.max(part)
        windows = (last - first) // WINDOW + 1
        work[0, c] = c
        work[1, c] = first

        def enter(w, n, c=c, first=first):
            work[0, n] = c
            work[1, n] = first + w * WINDOW
            return n + 1

        count = lax.fori_loop(1, windows, enter, count)
    work[2, 0] = count
    dense[...] = jnp.zeros_like(dense)

    def scatter(at, start):
        own = cells[:, at]
        kind = jnp.right_shift(words[:, at], 15).astype(jnp.float32)
        payload = jnp.where(depth_mask(own), kind, 0.0).astype(jnp.bfloat16)
        return product(column_hot(own, start), payload, NT)

    over_windows(work, scatter, window_adder(dense))
    load.wait()
    for k in range(5):
        face_up[k * WX : (k + 1) * WX, :] = resident[Y_UP[k], :, WY - 1, :]
        face_down[k * WX : (k + 1) * WX, :] = resident[Y_DOWN[k], :, 0, :]
    chosen[COLUMNS:] = jnp.zeros((PADDED_COLUMNS - COLUMNS, NZ), jnp.float32)

    def select(x, carry):
        rows = pl.ds(pl.multiple_of(x * WY, WY), WY)
        where = dense[rows, :]
        value = jnp.zeros((WY, NZ), jnp.float32)
        for i in range(1, 19):
            value = jnp.where(where == float(i), resident[i, x], value)
        chosen[rows, :] = value
        return carry

    lax.fori_loop(0, WX, select, 0, unroll=2)


def window_adder(dense):
    def add(at, start, value):
        dense[pl.ds(start, WINDOW), :] += value

    return add


def over_windows(work, compute, apply):
    for group in range(0, 8, 4):
        results = []
        for c in range(group, group + 4):
            at = slice(c * 1024, (c + 1) * 1024)
            start = pl.multiple_of(work[1, c], 8)
            results.append((at, start, compute(at, start)))
        for result in results:
            apply(*result)

    def step(n, carry):
        at = pl.ds(pl.multiple_of(work[0, n] * 1024, 1024), 1024)
        start = pl.multiple_of(work[1, n], 8)
        apply(at, start, compute(at, start))
        return carry

    lax.fori_loop(8, work[2, 0], step, 0)


def hbm():
    return pl.BlockSpec(memory_space=pltpu.HBM)


def smem():
    return pl.BlockSpec(memory_space=pltpu.SMEM)


def pick(sizes, cell, heading, floe, populations):
    links = cell.shape[0] * cell.shape[1]
    face = jax.ShapeDtypeStruct((FACE, 128), jnp.float32)
    row = jax.ShapeDtypeStruct((1, links), jnp.int32)
    return pl.pallas_call(
        functools.partial(pick_kernel, sizes),
        out_shape=(
            row,
            row,
            jax.ShapeDtypeStruct((3, 32), jnp.int32),
            jax.ShapeDtypeStruct((PADDED_COLUMNS, NZ), jnp.float32),
            jax.ShapeDtypeStruct((PADDED_COLUMNS, NZ), jnp.float32),
            face,
            face,
        ),
        in_specs=[whole(), whole(), whole(), hbm()],
        out_specs=(whole(), whole(), smem(), whole(), whole(), whole(), whole()),
        scratch_shapes=[
            pltpu.VMEM((128, 128), jnp.int32),
            pltpu.VMEM(populations.shape, jnp.float32),
            pltpu.SemaphoreType.DMA((1,)),
        ],
        compiler_params=params(48),
        cost_estimate=cost(7_000_000_000, 1_000_000),
        name="pick",
    )(cell, heading, floe, populations)


def gather_kernel(work, cell, chosen, out):
    out[...] = jnp.zeros_like(out)

    def read(at, start):
        own = cell[:, at]
        turned = jnp.transpose(chosen[pl.ds(start, WINDOW), :])
        high = turned.astype(jnp.bfloat16)
        low = (turned - high.astype(jnp.float32)).astype(jnp.bfloat16)
        values = product(jnp.concatenate([high, low], axis=0), column_hot(own, start), NN)
        values = values[0:NZ] + values[NZ : 2 * NZ]
        return jnp.sum(jnp.where(depth_mask(own), values, 0.0), axis=0, keepdims=True)

    def add(at, start, value):
        out[:, at] += value

    over_windows(work, read, add)


def gather(work, cell, chosen):
    return pl.pallas_call(
        gather_kernel,
        out_shape=jax.ShapeDtypeStruct(cell.shape, jnp.float32),
        in_specs=[smem(), whole(), whole()],
        out_specs=whole(),
        compiler_params=params(12),
        cost_estimate=cost(6_000_000_000, 2_000_000),
        name="gather",
    )(work, cell, chosen)


def bits(table, heading):
    word = 0
    for i in table:
        word |= 1 << i
    return jnp.bitwise_and(jnp.right_shift(jnp.full_like(heading, word), heading), 1)


def component(axis, heading):
    plus = [i for i in range(19) if DIRECTIONS[i][axis] == 1]
    minus = [i for i in range(19) if DIRECTIONS[i][axis] == -1]
    return (bits(plus, heading) - bits(minus, heading)).astype(jnp.float32)


def floe_kernel(
    cell, words, here, mine, low, high, left, right,
    taken, loads_left, loads_mid, loads_right, table, hot, spread, payload, total,
):
    links = cell.shape[1]
    for ra in range(3):
        for rb in range(3):
            if rb == 0:
                state = left[ra * STATE_ROWS : (ra + 1) * STATE_ROWS]
            elif rb == 2:
                state = right[ra * STATE_ROWS : (ra + 1) * STATE_ROWS]
            else:
                state = (low, mine, high)[ra][0:STATE_ROWS]
            region = ra * 3 + rb
            lanes = slice(region * 128, (region + 1) * 128)
            first = state.astype(jnp.bfloat16)
            table[0:STATE_ROWS, lanes] = first
            table[STATE_ROWS : 2 * STATE_ROWS, lanes] = (
                state - first.astype(jnp.float32)
            ).astype(jnp.bfloat16)
    payload[...] = jnp.zeros_like(payload)

    def first_half(t):
        slot = t % 2
        at = slice(t * CHUNK, (t + 1) * CHUNK)
        k = cell[:, at]
        word = words[:, at]
        d = jnp.right_shift(word, 15)
        place = jnp.bitwise_and(word, 32767)
        region = jnp.right_shift(place, 11)
        ra = jnp.right_shift(region * 11, 5)
        rb = region - 3 * ra
        group = jnp.bitwise_and(jnp.right_shift(place, 7), GROUPS - 1)
        entry = region * 128 + jnp.bitwise_and(place, 127)
        rows = lax.broadcasted_iota(jnp.int32, (9 * 128, CHUNK), 0)
        pick_floe = jnp.where(rows == entry, 1.0, 0.0).astype(jnp.bfloat16)
        groups = lax.broadcasted_iota(jnp.int32, (GROUPS, CHUNK), 0)
        mask = jnp.where(groups == group, 1.0, 0.0)

        cx = component(0, d)
        cy = component(1, d)
        cz = component(2, d)
        weight = jnp.where(d <= 6, WEIGHTS[1], WEIGHTS[7])
        lx = jnp.right_shift(k, 12)
        ly = jnp.bitwise_and(jnp.right_shift(k, 7), 31)
        lz = jnp.bitwise_and(k, 127)
        rx = ((1 - ra) * WX + lx).astype(jnp.float32) + 0.5 * cx
        ry = ((1 - rb) * WY + ly).astype(jnp.float32) + 0.5 * cy
        rz = lz.astype(jnp.float32) + 0.5 * cz
        scale = 1.0 / LEVER_SCALE
        coefficients = [
            cx,
            cy,
            cz,
            (ry * cz - rz * cy) * scale,
            (rz * cx - rx * cz) * scale,
            (rx * cy - ry * cx) * scale,
        ]
        for c in range(6):
            spread[slot, c * GROUPS : (c + 1) * GROUPS, :] = mask * coefficients[c]
        hot[slot] = pick_floe

        state = product(table[...], pick_floe, NN)
        state = state[0:STATE_ROWS] + state[STATE_ROWS : 2 * STATE_ROWS]
        weights = spread[slot]
        speed = jnp.sum(state * weights, axis=0, keepdims=True)
        take = (6.0 * FLOW_SCALE) * weight * speed
        magnitude = 2.0 * here[:, at] - take
        taken[:, at] = take
        amount = weights * magnitude
        first = amount.astype(jnp.bfloat16)
        payload[slot, 0:STATE_ROWS, :] = first
        payload[slot, 128 : 128 + STATE_ROWS, :] = (amount - first.astype(jnp.float32)).astype(
            jnp.bfloat16
        )

    def second_half(t):
        value = product(hot[t % 2], payload[t % 2], NT)
        if t == 0:
            total[...] = value
        else:
            total[...] += value

    steps = links // CHUNK
    first_half(0)
    for t in range(1, steps):
        first_half(t)
        second_half(t - 1)
    second_half(steps - 1)
    for ra in range(3):
        for rb in range(3):
            rows = slice((ra * 3 + rb) * 128, (ra * 3 + rb + 1) * 128)
            summed = total[rows, 0:128] + total[rows, 128:256]
            out = (loads_left, loads_mid, loads_right)[rb]
            out[ra * STATE_ROWS : (ra + 1) * STATE_ROWS] = jnp.transpose(summed)[0:STATE_ROWS]


def floes(cell, words, here, mine, low, high, left, right):
    loads = jax.ShapeDtypeStruct((3 * STATE_ROWS, 128), jnp.float32)
    return pl.pallas_call(
        floe_kernel,
        out_shape=(jax.ShapeDtypeStruct(cell.shape, jnp.float32), loads, loads, loads),
        in_specs=[whole()] * 8,
        out_specs=(whole(),) * 4,
        scratch_shapes=[
            pltpu.VMEM((2 * STATE_ROWS, 9 * 128), jnp.bfloat16),
            pltpu.VMEM((2, 9 * 128, CHUNK), jnp.bfloat16),
            pltpu.VMEM((2, STATE_ROWS, CHUNK), jnp.float32),
            pltpu.VMEM((2, 256, CHUNK), jnp.bfloat16),
            pltpu.VMEM((9 * 128, 256), jnp.float32),
        ],
        compiler_params=params(18),
        cost_estimate=cost(8_000_000_000, 2_000_000),
        name="floes",
    )(cell, words, here, mine, low, high, left, right)


def spread_kernel(work, cell, taken, dense):
    dense[...] = jnp.zeros_like(dense)

    def scatter(at, start):
        own = cell[:, at]
        value = taken[:, at]
        first = value.astype(jnp.bfloat16).astype(jnp.float32)
        mask = depth_mask(own)
        payload = jnp.concatenate(
            [
                jnp.where(mask, first, 0.0).astype(jnp.bfloat16),
                jnp.where(mask, value - first, 0.0).astype(jnp.bfloat16),
            ],
            axis=0,
        )
        both = product(column_hot(own, start), payload, NT)
        return both[:, :NZ] + both[:, NZ:]

    over_windows(work, scatter, window_adder(dense))


def spread_out(work, cell, taken):
    return pl.pallas_call(
        spread_kernel,
        out_shape=jax.ShapeDtypeStruct((PADDED_COLUMNS, NZ), jnp.float32),
        in_specs=[smem(), whole(), whole()],
        out_specs=whole(),
        compiler_params=params(8),
        cost_estimate=cost(3_000_000_000, 1_000_000),
        name="spread",
    )(work, cell, taken)


SLAB = 2
SLOTS = 4
SLABS = WX // SLAB
TOP = 8


def collide_kernel(
    dense_dir, dense_take, low, high, left, right, pop_hbm, out_hbm, pop, out, load_sem, store_sem
):
    def loading(s):
        return pltpu.make_async_copy(
            pop_hbm.at[:, pl.ds(s * SLAB, SLAB)],
            pop.at[:, pl.ds(1 + s * SLAB, SLAB), pl.ds(TOP, WY), :],
            load_sem.at[s],
        )

    for s in range(SLABS):
        loading(s).start()
    for k in range(5):
        rows = slice(STATE_ROWS + k * WY, STATE_ROWS + (k + 1) * WY)
        pop[X_UP[k], 0, TOP : TOP + WY, :] = low[rows, :]
        pop[X_DOWN[k], WX + 1, TOP : TOP + WY, :] = high[rows, :]
    base = 3 * STATE_ROWS
    for k in range(5):
        for x in range(WX):
            row = base + k * WX + x
            pop[Y_UP[k], 1 + x, TOP - 1 : TOP, :] = left[row : row + 1, :]
            pop[Y_DOWN[k], 1 + x, TOP + WY : TOP + WY + 1, :] = right[row : row + 1, :]
    edge = base + FACE
    pop[7, 0, TOP - 1 : TOP, :] = left[edge : edge + 1, :]
    pop[10, WX + 1, TOP - 1 : TOP, :] = left[edge + 1 : edge + 2, :]
    pop[9, 0, TOP + WY : TOP + WY + 1, :] = right[edge : edge + 1, :]
    pop[8, WX + 1, TOP + WY : TOP + WY + 1, :] = right[edge + 1 : edge + 2, :]

    def storing(s, slot):
        return pltpu.make_async_copy(
            out.at[slot], out_hbm.at[:, pl.ds(s * SLAB, SLAB)], store_sem.at[slot]
        )

    lane = lax.broadcasted_iota(jnp.int32, (8, 128), 1)
    first_lane = lane == 0
    last_lane = lane == NZ - 1
    rest = 1.0 - RELAXATION

    def tile(x, j, slot, inner):
        row = pl.multiple_of(x * WY, WY) + j * 8
        where = dense_dir[pl.ds(row, 8), :]
        take = dense_take[pl.ds(row, 8), :]

        def plain(i):
            return pop[i, x + 1, TOP + j * 8 : TOP + j * 8 + 8, :]

        def bounded(i, back):
            step_x, step_y, step_z = DIRECTIONS[i]
            start = TOP + j * 8 - step_y
            value = pop[i, x + 1 - step_x, start : start + 8, :]
            if step_z == 1:
                value = jnp.where(first_lane, back, pltpu.roll(value, 1, 1))
            elif step_z == -1:
                value = jnp.where(last_lane, back, pltpu.roll(value, NZ - 1, 1))
            return jnp.where(where == float(opposite(i)), back - take, value)

        centre = plain(0)
        density = centre
        both = []
        apart = []
        for i in range(1, 19, 2):
            plus = bounded(i, plain(i + 1))
            minus = bounded(i + 1, plain(i))
            both.append((plus, minus))
            apart.append(plus - minus)
            density = density + (plus + minus)
        d1, d3, d5, d7, d9, d11, d13, d15, d17 = apart
        mx = (d3 + d7) + (d9 + d11) + d13
        my = (d5 + d7) + (d15 - d9) + d17
        mz = (d1 + d11) + (d15 - d13) - d17
        inverse = 1.0 / density
        ux = mx * inverse
        uy = my * inverse
        uz = mz * inverse
        scaled = density * RELAXATION
        flat = scaled * (1.0 - 1.5 * (ux * ux + uy * uy + uz * uz))
        linear = 3.0 * scaled
        square = 4.5 * scaled
        out[slot, 0, inner, j * 8 : j * 8 + 8, :] = rest * centre + WEIGHTS[0] * flat
        for n in range(9):
            i = 2 * n + 1
            step_x, step_y, step_z = DIRECTIONS[i]
            projection = None
            for step, u in ((step_x, ux), (step_y, uy), (step_z, uz)):
                if step == 0:
                    continue
                if projection is None:
                    projection = u
                else:
                    projection = projection + u if step == 1 else projection - u
            even = WEIGHTS[i] * (flat + square * (projection * projection))
            odd = WEIGHTS[i] * (linear * projection)
            plus, minus = both[n]
            out[slot, i, inner, j * 8 : j * 8 + 8, :] = rest * plus + (even + odd)
            out[slot, i + 1, inner, j * 8 : j * 8 + 8, :] = rest * minus + (even - odd)

    loading(0).wait()

    def slab(s, carry):
        slot = lax.rem(s, SLOTS)

        @pl.when(s + 1 < SLABS)
        def _():
            loading(s + 1).wait()

        @pl.when(s >= SLOTS)
        def _():
            storing(s - SLOTS, slot).wait()

        def plane(inner, inside):
            for j in range(WY // 8):
                tile(s * SLAB + inner, j, slot, inner)
            return inside

        lax.fori_loop(0, SLAB, plane, 0)
        storing(s, slot).start()
        return carry

    lax.fori_loop(0, SLABS, slab, 0)
    for s in range(SLABS - SLOTS, SLABS):
        storing(s, s % SLOTS).wait()


def collide(dense_dir, dense_take, low, high, left, right, populations):
    return pl.pallas_call(
        collide_kernel,
        out_shape=jax.ShapeDtypeStruct(populations.shape, jnp.float32),
        in_specs=[whole()] * 6 + [anywhere()],
        out_specs=anywhere(),
        scratch_shapes=[
            pltpu.VMEM((19, WX + 2, WY + 16, NZ), jnp.float32),
            pltpu.VMEM((SLOTS, 19, SLAB, WY, NZ), jnp.float32),
            pltpu.SemaphoreType.DMA((SLABS,)),
            pltpu.SemaphoreType.DMA((SLOTS,)),
        ],
        compiler_params=params(30),
        cost_estimate=cost(40_000_000, 24_000_000),
        name="collide",
    )(dense_dir, dense_take, low, high, left, right, populations)


def fold_kernel(dense, mid, left, right, own, to_low, to_high):
    def total(k):
        rows = slice(k * STATE_ROWS, (k + 1) * STATE_ROWS)
        return mid[rows] + (left[rows] + right[rows])

    to_low[...] = total(0)
    own[...] = total(1)
    to_high[...] = total(2)


def fold(dense, mid, left, right):
    shape = jax.ShapeDtypeStruct((STATE_ROWS, 128), jnp.float32)
    return pl.pallas_call(
        fold_kernel,
        out_shape=(shape,) * 3,
        in_specs=[anywhere(), whole(), whole(), whole()],
        out_specs=(whole(),) * 3,
        compiler_params=params(4),
        cost_estimate=cost(100_000, 600_000),
        name="fold",
    )(dense, mid, left, right)


def motion_kernel(own, low, high, place, velocity, response, out):
    loads = own[...] + low[...] + high[...]
    px, py, pz = origin_terms(place, velocity)
    scale = 1.0 / LEVER_SCALE
    for b in range(GROUPS):
        lanes = slice(b * 128, (b + 1) * 128)

        def load(c):
            return loads[c * GROUPS + b : c * GROUPS + b + 1, :]

        fx, fy, fz = load(0), load(1), load(2)
        qx, qy, qz = px[:, lanes], py[:, lanes], pz[:, lanes]
        torques = [
            load(3) - (qy * fz - qz * fy) * scale,
            load(4) - (qz * fx - qx * fz) * scale,
            load(5) - (qx * fy - qy * fx) * scale,
        ]
        for c, value in enumerate((fx, fy, fz)):
            out[c : c + 1, lanes] = velocity[c : c + 1, lanes] + response[0:1, lanes] * value
        for c, value in enumerate(torques):
            out[c + 3 : c + 4, lanes] = (
                velocity[c + 3 : c + 4, lanes] + response[1:2, lanes] * value
            )


def motion(own, low, high, place, velocity, response):
    return pl.pallas_call(
        motion_kernel,
        out_shape=jax.ShapeDtypeStruct(velocity.shape, jnp.float32),
        in_specs=[whole()] * 6,
        out_specs=whole(),
        compiler_params=params(4),
        cost_estimate=cost(200_000, 300_000),
        name="motion",
    )(own, low, high, place, velocity, response)


def shifted(value, axis, step):
    count = lax.axis_size(axis)
    return lax.ppermute(value, axis, [(i, (i + step) % count) for i in range(count)])


def body(populations, link_cell, link_dir, link_floe, floe_place, floe_velocity, floe_response):
    sizes = (lax.axis_size("along"), lax.axis_size("across"))
    links = link_cell.shape[-1]
    cell = link_cell.reshape(links // 128, 128)
    heading = link_dir.reshape(links // 128, 128)
    floe = link_floe.reshape(links // 128, 128)

    up, down = prepare(floe_place, floe_velocity, populations)
    low = shifted(up, "along", 1)
    high = shifted(down, "along", -1)
    cells, words, work, dense_dir, chosen, face_up, face_down = pick(
        sizes, cell, heading, floe, populations
    )

    def rows(block, k, y):
        at = STATE_ROWS + k * WY + y
        return block[at : at + 1]

    states = [low[:STATE_ROWS], up[:STATE_ROWS], high[:STATE_ROWS]]
    filler = jnp.zeros((EDGE_ROWS - 2, 128), jnp.float32)
    to_up = jnp.concatenate(
        states + [face_up, rows(low, X_UP.index(7), WY - 1), rows(high, X_DOWN.index(10), WY - 1)]
        + [filler]
    )
    to_down = jnp.concatenate(
        states + [face_down, rows(low, X_UP.index(9), 0), rows(high, X_DOWN.index(8), 0), filler]
    )
    left = shifted(to_up, "across", 1)
    right = shifted(to_down, "across", -1)
    here = gather(work, cells, chosen)
    taken, loads_left, loads_mid, loads_right = floes(
        cells, words, here, up, low, high, left, right
    )
    from_right = shifted(loads_left, "across", -1)
    from_left = shifted(loads_right, "across", 1)
    dense_take = spread_out(work, cells, taken)
    own, to_low, to_high = fold(dense_take, loads_mid, from_left, from_right)
    from_high = shifted(to_low, "along", -1)
    from_low = shifted(to_high, "along", 1)
    relaxed = collide(dense_dir, dense_take, low, high, left, right, populations)
    moved = motion(
        own,
        from_low,
        from_high,
        floe_place,
        floe_velocity,
        floe_response,
    )
    return relaxed, moved


def solution(mesh):
    placed = (
        P(None, "along", "across", None),
        P("along", "across", None),
        P("along", "across", None),
        P("along", "across", None),
        P(None, ("along", "across")),
        P(None, ("along", "across")),
        P(None, ("along", "across")),
    )
    return jax.shard_map(
        body,
        mesh=mesh,
        in_specs=placed,
        out_specs=(P(None, "along", "across", None), P(None, ("along", "across"))),
        check_vma=False,
    )
```

```python
import functools

import jax
import jax.numpy as jnp
from jax import lax
from jax.experimental import pallas as pl
from jax.experimental.pallas import tpu as pltpu
from jax.sharding import PartitionSpec as P

DIRECTIONS = [
    (0, 0, 0),
    (0, 0, 1),
    (0, 0, -1),
    (1, 0, 0),
    (-1, 0, 0),
    (0, 1, 0),
    (0, -1, 0),
    (1, 1, 0),
    (-1, -1, 0),
    (1, -1, 0),
    (-1, 1, 0),
    (1, 0, 1),
    (-1, 0, -1),
    (1, 0, -1),
    (-1, 0, 1),
    (0, 1, 1),
    (0, -1, -1),
    (0, 1, -1),
    (0, -1, 1),
]
WEIGHTS = [1.0 / 3.0] + [1.0 / 18.0] * 6 + [1.0 / 36.0] * 12
RELAXATION = 1.0 / 0.6
FLOW_SCALE = 0.02
LEVER_SCALE = 64.0

WX = 32
WY = 32
NZ = 128
COLUMNS = WX * WY
MEMBERS = 2048
GROUPS = MEMBERS // 128
STATE_ROWS = 6 * GROUPS
FACE = 5 * WX
EDGE_ROWS = 8
WINDOW = 160
PADDED_COLUMNS = COLUMNS + WINDOW
CHUNK = 1024

X_UP = [i for i in range(19) if DIRECTIONS[i][0] == 1]
X_DOWN = [i for i in range(19) if DIRECTIONS[i][0] == -1]
Y_UP = [i for i in range(19) if DIRECTIONS[i][1] == 1]
Y_DOWN = [i for i in range(19) if DIRECTIONS[i][1] == -1]


def opposite(i):
    if i == 0:
        return 0
    return i + 1 if i % 2 == 1 else i - 1


def params(mebibytes):
    return pltpu.CompilerParams(vmem_limit_bytes=mebibytes * 1024 * 1024)


def cost(flops, moved):
    return pl.CostEstimate(flops=flops, bytes_accessed=moved, transcendentals=0)


def whole():
    return pl.BlockSpec(memory_space=pltpu.VMEM)


def anywhere():
    return pl.BlockSpec(memory_space=pl.ANY)


def origin_terms(place, velocity):
    px = place[0:1] * float(WX)
    py = place[1:2] * float(WY)
    pz = place[2:3] * float(NZ)
    return px, py, pz


def prepare_kernel(
    place_hbm, velocity_hbm, pop, up, down, place, velocity, sem, small_sem
):
    small = [
        pltpu.make_async_copy(place_hbm, place, small_sem.at[0]),
        pltpu.make_async_copy(velocity_hbm, velocity, small_sem.at[1]),
    ]
    for copy in small:
        copy.start()
    copies = []
    for k in range(5):
        rows = pl.ds(STATE_ROWS + k * WY, WY)
        copies.append(pltpu.make_async_copy(pop.at[X_UP[k], WX - 1], up.at[rows, :], sem.at[0]))
        copies.append(pltpu.make_async_copy(pop.at[X_DOWN[k], 0], down.at[rows, :], sem.at[0]))
    for copy in copies:
        copy.start()
    for copy in small:
        copy.wait()
    px, py, pz = origin_terms(place, velocity)
    wx, wy, wz = velocity[3:4], velocity[4:5], velocity[5:6]
    scale = 1.0 / LEVER_SCALE
    values = [
        velocity[0:1] - (wy * pz - wz * py) * scale,
        velocity[1:2] - (wz * px - wx * pz) * scale,
        velocity[2:3] - (wx * py - wy * px) * scale,
        wx,
        wy,
        wz,
    ]
    for c in range(6):
        for b in range(GROUPS):
            row = values[c][:, b * 128 : (b + 1) * 128]
            up[c * GROUPS + b : c * GROUPS + b + 1, :] = row
            down[c * GROUPS + b : c * GROUPS + b + 1, :] = row
    for copy in copies:
        copy.wait()


def prepare(place, velocity, populations):
    shape = jax.ShapeDtypeStruct((STATE_ROWS + FACE, 128), jnp.float32)
    return pl.pallas_call(
        prepare_kernel,
        out_shape=(shape, shape),
        in_specs=[hbm(), hbm(), hbm()],
        out_specs=(whole(),) * 2,
        scratch_shapes=[
            pltpu.VMEM(place.shape, jnp.float32),
            pltpu.VMEM(velocity.shape, jnp.float32),
            pltpu.SemaphoreType.DMA((1,)),
            pltpu.SemaphoreType.DMA((2,)),
        ],
        compiler_params=params(58),
        cost_estimate=cost(100_000, 2_600_000),
        name="prepare",
    )(place, velocity, populations)


NT = (((1,), (1,)), ((), ()))
NN = (((1,), (0,)), ((), ()))


def product(a, b, dims):
    return lax.dot_general(a, b, dims, preferred_element_type=jnp.float32)


def column_hot(cell, start):
    rows = lax.broadcasted_iota(jnp.int32, (WINDOW, cell.shape[1]), 0)
    return jnp.where(rows == jnp.right_shift(cell, 7) - start, 1.0, 0.0).astype(jnp.bfloat16)


def depth_mask(cell):
    rows = lax.broadcasted_iota(jnp.int32, (NZ, cell.shape[1]), 0)
    return rows == jnp.bitwise_and(cell, NZ - 1)


def sorted_chunks(keys, values):
    lane = lax.broadcasted_iota(jnp.int32, (8, 128), 1)
    sublane = lax.broadcasted_iota(jnp.int32, (8, 128), 0)

    def bit(position):
        if position < 6:
            return jnp.bitwise_and(jnp.right_shift(sublane, position - 3), 1)
        return jnp.bitwise_and(jnp.right_shift(lane, position - 6), 1)

    def partner(x, position):
        axis = 0 if position < 6 else 1
        extent = x.shape[axis]
        distance = 1 << (position - (3 if position < 6 else 6))
        if 2 * distance == extent:
            return pltpu.roll(x, distance, axis)
        return jnp.where(
            bit(position) == 0,
            pltpu.roll(x, extent - distance, axis),
            pltpu.roll(x, distance, axis),
        )

    for merge in range(1, 14):
        for position in range(merge - 1, -1, -1):
            if merge == 13 and position < 10:
                continue
            if position < 3:
                for v in range(8):
                    u = v | (1 << position)
                    if u == v:
                        continue
                    below = keys[u] < keys[v]
                    if merge < 3:
                        if (v >> merge) & 1:
                            below = keys[u] > keys[v]
                    elif merge < 13:
                        below = jnp.logical_xor(below, bit(merge) == 1)
                    keys[v], keys[u] = (
                        jnp.where(below, keys[u], keys[v]),
                        jnp.where(below, keys[v], keys[u]),
                    )
                    values[v], values[u] = (
                        jnp.where(below, values[u], values[v]),
                        jnp.where(below, values[v], values[u]),
                    )
                continue
            if merge < 13:
                least = bit(position) == bit(merge)
            else:
                least = bit(position) == 0
            for v in range(8):
                other = partner(keys[v], position)
                carried = partner(values[v], position)
                stay = jnp.logical_xor(other < keys[v], least)
                keys[v] = jnp.where(stay, keys[v], other)
                values[v] = jnp.where(stay, values[v], carried)
    return keys, values


def pick_kernel(
    sizes, cell, heading, floe, pop, cells, words, work, dense, chosen, face_up, face_down,
    turned, resident, sem,
):
    load = pltpu.make_async_copy(pop, resident, sem.at[0])
    load.start()
    size_along, size_across = sizes
    a = lax.axis_index("along")
    b = lax.axis_index("across")
    keys = []
    values = []
    for v in range(8):
        rows = slice(v * 8, (v + 1) * 8)
        g = floe[rows, :]
        owner = jnp.right_shift(g, 11)
        ra = jnp.bitwise_and(owner // size_across - a + 1, size_along - 1)
        rb = jnp.bitwise_and(jnp.bitwise_and(owner, size_across - 1) - b + 1, size_across - 1)
        entry = (ra * 3 + rb) * MEMBERS + jnp.bitwise_and(g, MEMBERS - 1)
        word = jnp.left_shift(heading[rows, :], 15) + entry
        keys.append(cell[rows, :])
        values.append(jnp.where(g >= 0, word, 9 * MEMBERS))
    keys, values = sorted_chunks(keys, values)
    turned[...] = jnp.transpose(jnp.concatenate(keys + values, axis=0))
    even = turned[pl.ds(0, 64, stride=2), :]
    odd = turned[pl.ds(1, 64, stride=2), :]
    left = lax.broadcasted_iota(jnp.int32, (64, 128), 1) < 64
    key = jnp.where(left, even, pltpu.roll(odd, 64, 1))
    value = jnp.where(left, pltpu.roll(even, 64, 1), odd)
    for r in range(64):
        cells[:, r * 128 : (r + 1) * 128] = key[r : r + 1, :]
        words[:, r * 128 : (r + 1) * 128] = value[r : r + 1, :]
    column = jnp.right_shift(key, 7)
    count = jnp.int32(8)
    for c in range(8):
        part = column[c * 8 : (c + 1) * 8, :]
        first = jnp.left_shift(jnp.right_shift(jnp.min(part), 3), 3)
        last = jnp.max(part)
        windows = (last - first) // WINDOW + 1
        work[0, c] = c
        work[1, c] = first

        def enter(w, n, c=c, first=first):
            work[0, n] = c
            work[1, n] = first + w * WINDOW
            return n + 1

        count = lax.fori_loop(1, windows, enter, count)
    work[2, 0] = count
    dense[...] = jnp.zeros_like(dense)

    def scatter(at, start):
        own = cells[:, at]
        kind = jnp.right_shift(words[:, at], 15).astype(jnp.float32)
        payload = jnp.where(depth_mask(own), kind, 0.0).astype(jnp.bfloat16)
        return product(column_hot(own, start), payload, NT)

    over_windows(work, scatter, window_adder(dense))
    load.wait()
    for k in range(5):
        face_up[k * WX : (k + 1) * WX, :] = resident[Y_UP[k], :, WY - 1, :]
        face_down[k * WX : (k + 1) * WX, :] = resident[Y_DOWN[k], :, 0, :]
    chosen[COLUMNS:] = jnp.zeros((PADDED_COLUMNS - COLUMNS, NZ), jnp.float32)

    def select(x, carry):
        rows = pl.ds(pl.multiple_of(x * WY, WY), WY)
        where = dense[rows, :]
        value = jnp.zeros((WY, NZ), jnp.float32)
        for i in range(1, 19):
            value = jnp.where(where == float(i), resident[i, x], value)
        chosen[rows, :] = value
        return carry

    lax.fori_loop(0, WX, select, 0, unroll=2)


def window_adder(dense):
    def add(at, start, value):
        dense[pl.ds(start, WINDOW), :] += value

    return add


def over_windows(work, compute, apply):
    for group in range(0, 8, 4):
        results = []
        for c in range(group, group + 4):
            at = slice(c * 1024, (c + 1) * 1024)
            start = pl.multiple_of(work[1, c], 8)
            results.append((at, start, compute(at, start)))
        for result in results:
            apply(*result)

    def step(n, carry):
        at = pl.ds(pl.multiple_of(work[0, n] * 1024, 1024), 1024)
        start = pl.multiple_of(work[1, n], 8)
        apply(at, start, compute(at, start))
        return carry

    lax.fori_loop(8, work[2, 0], step, 0)


def hbm():
    return pl.BlockSpec(memory_space=pltpu.HBM)


def smem():
    return pl.BlockSpec(memory_space=pltpu.SMEM)


def pick(sizes, cell, heading, floe, populations):
    links = cell.shape[0] * cell.shape[1]
    face = jax.ShapeDtypeStruct((FACE, 128), jnp.float32)
    row = jax.ShapeDtypeStruct((1, links), jnp.int32)
    return pl.pallas_call(
        functools.partial(pick_kernel, sizes),
        out_shape=(
            row,
            row,
            jax.ShapeDtypeStruct((3, 32), jnp.int32),
            jax.ShapeDtypeStruct((PADDED_COLUMNS, NZ), jnp.float32),
            jax.ShapeDtypeStruct((PADDED_COLUMNS, NZ), jnp.float32),
            face,
            face,
        ),
        in_specs=[whole(), whole(), whole(), hbm()],
        out_specs=(whole(), whole(), smem(), whole(), whole(), whole(), whole()),
        scratch_shapes=[
            pltpu.VMEM((128, 128), jnp.int32),
            pltpu.VMEM(populations.shape, jnp.float32),
            pltpu.SemaphoreType.DMA((1,)),
        ],
        compiler_params=params(48),
        cost_estimate=cost(7_000_000_000, 1_000_000),
        name="pick",
    )(cell, heading, floe, populations)


def gather_kernel(work, cell, chosen, out):
    out[...] = jnp.zeros_like(out)

    def read(at, start):
        own = cell[:, at]
        turned = jnp.transpose(chosen[pl.ds(start, WINDOW), :])
        high = turned.astype(jnp.bfloat16)
        low = (turned - high.astype(jnp.float32)).astype(jnp.bfloat16)
        values = product(jnp.concatenate([high, low], axis=0), column_hot(own, start), NN)
        values = values[0:NZ] + values[NZ : 2 * NZ]
        return jnp.sum(jnp.where(depth_mask(own), values, 0.0), axis=0, keepdims=True)

    def add(at, start, value):
        out[:, at] += value

    over_windows(work, read, add)


def gather(work, cell, chosen):
    return pl.pallas_call(
        gather_kernel,
        out_shape=jax.ShapeDtypeStruct(cell.shape, jnp.float32),
        in_specs=[smem(), whole(), whole()],
        out_specs=whole(),
        compiler_params=params(12),
        cost_estimate=cost(6_000_000_000, 2_000_000),
        name="gather",
    )(work, cell, chosen)


def bits(table, heading):
    word = 0
    for i in table:
        word |= 1 << i
    return jnp.bitwise_and(jnp.right_shift(jnp.full_like(heading, word), heading), 1)


def component(axis, heading):
    plus = [i for i in range(19) if DIRECTIONS[i][axis] == 1]
    minus = [i for i in range(19) if DIRECTIONS[i][axis] == -1]
    return (bits(plus, heading) - bits(minus, heading)).astype(jnp.float32)


def floe_kernel(
    cell, words, here, mine, low, high, left, right,
    taken, loads_left, loads_mid, loads_right, table, hot, spread, payload, total,
):
    links = cell.shape[1]
    for ra in range(3):
        for rb in range(3):
            if rb == 0:
                state = left[ra * STATE_ROWS : (ra + 1) * STATE_ROWS]
            elif rb == 2:
                state = right[ra * STATE_ROWS : (ra + 1) * STATE_ROWS]
            else:
                state = (low, mine, high)[ra][0:STATE_ROWS]
            region = ra * 3 + rb
            lanes = slice(region * 128, (region + 1) * 128)
            first = state.astype(jnp.bfloat16)
            table[0:STATE_ROWS, lanes] = first
            table[STATE_ROWS : 2 * STATE_ROWS, lanes] = (
                state - first.astype(jnp.float32)
            ).astype(jnp.bfloat16)
    def first_half(t):
        slot = t % 2
        at = slice(t * CHUNK, (t + 1) * CHUNK)
        k = cell[:, at]
        word = words[:, at]
        d = jnp.right_shift(word, 15)
        place = jnp.bitwise_and(word, 32767)
        region = jnp.right_shift(place, 11)
        ra = jnp.right_shift(region * 11, 5)
        rb = region - 3 * ra
        group = jnp.bitwise_and(jnp.right_shift(place, 7), GROUPS - 1)
        entry = region * 128 + jnp.bitwise_and(place, 127)
        rows = lax.broadcasted_iota(jnp.int32, (9 * 128, CHUNK), 0)
        pick_floe = jnp.where(rows == entry, 1.0, 0.0).astype(jnp.bfloat16)
        groups = lax.broadcasted_iota(jnp.int32, (GROUPS, CHUNK), 0)
        mask = jnp.where(groups == group, 1.0, 0.0)

        cx = component(0, d)
        cy = component(1, d)
        cz = component(2, d)
        weight = jnp.where(d <= 6, WEIGHTS[1], WEIGHTS[7])
        lx = jnp.right_shift(k, 12)
        ly = jnp.bitwise_and(jnp.right_shift(k, 7), 31)
        lz = jnp.bitwise_and(k, 127)
        rx = ((1 - ra) * WX + lx).astype(jnp.float32) + 0.5 * cx
        ry = ((1 - rb) * WY + ly).astype(jnp.float32) + 0.5 * cy
        rz = lz.astype(jnp.float32) + 0.5 * cz
        scale = 1.0 / LEVER_SCALE
        coefficients = [
            cx,
            cy,
            cz,
            (ry * cz - rz * cy) * scale,
            (rz * cx - rx * cz) * scale,
            (rx * cy - ry * cx) * scale,
        ]
        for c in range(6):
            spread[slot, c * GROUPS : (c + 1) * GROUPS, :] = mask * coefficients[c]
        hot[slot] = pick_floe

        state = product(table[...], pick_floe, NN)
        state = state[0:STATE_ROWS] + state[STATE_ROWS : 2 * STATE_ROWS]
        weights = spread[slot]
        speed = jnp.sum(state * weights, axis=0, keepdims=True)
        take = (6.0 * FLOW_SCALE) * weight * speed
        magnitude = 2.0 * here[:, at] - take
        taken[:, at] = take
        amount = weights * magnitude
        first = amount.astype(jnp.bfloat16)
        payload[slot, 0:STATE_ROWS, :] = first
        payload[slot, STATE_ROWS : 2 * STATE_ROWS, :] = (amount - first.astype(jnp.float32)).astype(
            jnp.bfloat16
        )

    def second_half(t):
        value = product(payload[t % 2], hot[t % 2], NT)
        if t == 0:
            total[...] = value
        else:
            total[...] += value

    steps = links // CHUNK
    first_half(0)
    for t in range(1, steps):
        first_half(t)
        second_half(t - 1)
    second_half(steps - 1)
    for ra in range(3):
        for rb in range(3):
            lanes = slice((ra * 3 + rb) * 128, (ra * 3 + rb + 1) * 128)
            summed = total[0:STATE_ROWS, lanes] + total[STATE_ROWS : 2 * STATE_ROWS, lanes]
            out = (loads_left, loads_mid, loads_right)[rb]
            out[ra * STATE_ROWS : (ra + 1) * STATE_ROWS] = summed


def floes(cell, words, here, mine, low, high, left, right):
    loads = jax.ShapeDtypeStruct((3 * STATE_ROWS, 128), jnp.float32)
    return pl.pallas_call(
        floe_kernel,
        out_shape=(jax.ShapeDtypeStruct(cell.shape, jnp.float32), loads, loads, loads),
        in_specs=[whole()] * 8,
        out_specs=(whole(),) * 4,
        scratch_shapes=[
            pltpu.VMEM((2 * STATE_ROWS, 9 * 128), jnp.bfloat16),
            pltpu.VMEM((2, 9 * 128, CHUNK), jnp.bfloat16),
            pltpu.VMEM((2, STATE_ROWS, CHUNK), jnp.float32),
            pltpu.VMEM((2, 2 * STATE_ROWS, CHUNK), jnp.bfloat16),
            pltpu.VMEM((2 * STATE_ROWS, 9 * 128), jnp.float32),
        ],
        compiler_params=params(18),
        cost_estimate=cost(8_000_000_000, 2_000_000),
        name="floes",
    )(cell, words, here, mine, low, high, left, right)


def spread_kernel(work, cell, taken, dense):
    dense[...] = jnp.zeros_like(dense)

    def scatter(at, start):
        own = cell[:, at]
        value = taken[:, at]
        first = value.astype(jnp.bfloat16).astype(jnp.float32)
        mask = depth_mask(own)
        payload = jnp.concatenate(
            [
                jnp.where(mask, first, 0.0).astype(jnp.bfloat16),
                jnp.where(mask, value - first, 0.0).astype(jnp.bfloat16),
            ],
            axis=0,
        )
        both = product(column_hot(own, start), payload, NT)
        return both[:, :NZ] + both[:, NZ:]

    over_windows(work, scatter, window_adder(dense))


def spread_out(work, cell, taken):
    return pl.pallas_call(
        spread_kernel,
        out_shape=jax.ShapeDtypeStruct((PADDED_COLUMNS, NZ), jnp.float32),
        in_specs=[smem(), whole(), whole()],
        out_specs=whole(),
        compiler_params=params(8),
        cost_estimate=cost(3_000_000_000, 1_000_000),
        name="spread",
    )(work, cell, taken)


SLAB = 2
SLOTS = 4
SLABS = WX // SLAB
TOP = 8


def collide_kernel(
    dense_dir, dense_take, low, high, left, right, pop_hbm, out_hbm, pop, out, load_sem, store_sem
):
    def loading(s):
        return pltpu.make_async_copy(
            pop_hbm.at[:, pl.ds(s * SLAB, SLAB)],
            pop.at[:, pl.ds(1 + s * SLAB, SLAB), pl.ds(TOP, WY), :],
            load_sem.at[s],
        )

    for s in range(SLABS):
        loading(s).start()
    for k in range(5):
        rows = slice(STATE_ROWS + k * WY, STATE_ROWS + (k + 1) * WY)
        pop[X_UP[k], 0, TOP : TOP + WY, :] = low[rows, :]
        pop[X_DOWN[k], WX + 1, TOP : TOP + WY, :] = high[rows, :]
    base = 3 * STATE_ROWS
    for k in range(5):
        for x in range(WX):
            row = base + k * WX + x
            pop[Y_UP[k], 1 + x, TOP - 1 : TOP, :] = left[row : row + 1, :]
            pop[Y_DOWN[k], 1 + x, TOP + WY : TOP + WY + 1, :] = right[row : row + 1, :]
    edge = base + FACE
    pop[7, 0, TOP - 1 : TOP, :] = left[edge : edge + 1, :]
    pop[10, WX + 1, TOP - 1 : TOP, :] = left[edge + 1 : edge + 2, :]
    pop[9, 0, TOP + WY : TOP + WY + 1, :] = right[edge : edge + 1, :]
    pop[8, WX + 1, TOP + WY : TOP + WY + 1, :] = right[edge + 1 : edge + 2, :]

    def storing(s, slot):
        return pltpu.make_async_copy(
            out.at[slot], out_hbm.at[:, pl.ds(s * SLAB, SLAB)], store_sem.at[slot]
        )

    lane = lax.broadcasted_iota(jnp.int32, (8, 128), 1)
    first_lane = lane == 0
    last_lane = lane == NZ - 1
    rest = 1.0 - RELAXATION

    def tile(x, j, slot, inner):
        row = pl.multiple_of(x * WY, WY) + j * 8
        where = dense_dir[pl.ds(row, 8), :]
        take = dense_take[pl.ds(row, 8), :]

        def plain(i):
            return pop[i, x + 1, TOP + j * 8 : TOP + j * 8 + 8, :]

        def bounded(i, back):
            step_x, step_y, step_z = DIRECTIONS[i]
            start = TOP + j * 8 - step_y
            value = pop[i, x + 1 - step_x, start : start + 8, :]
            if step_z == 1:
                value = jnp.where(first_lane, back, pltpu.roll(value, 1, 1))
            elif step_z == -1:
                value = jnp.where(last_lane, back, pltpu.roll(value, NZ - 1, 1))
            return jnp.where(where == float(opposite(i)), back - take, value)

        centre = plain(0)
        density = centre
        both = []
        apart = []
        for i in range(1, 19, 2):
            plus = bounded(i, plain(i + 1))
            minus = bounded(i + 1, plain(i))
            both.append((plus, minus))
            apart.append(plus - minus)
            density = density + (plus + minus)
        d1, d3, d5, d7, d9, d11, d13, d15, d17 = apart
        mx = (d3 + d7) + (d9 + d11) + d13
        my = (d5 + d7) + (d15 - d9) + d17
        mz = (d1 + d11) + (d15 - d13) - d17
        inverse = 1.5 / density
        ux = mx * inverse
        uy = my * inverse
        uz = mz * inverse
        scaled = density * RELAXATION
        flat = scaled - (2.0 / 3.0) * scaled * (ux * ux + uy * uy + uz * uz)
        parts = {w: (flat * w, scaled * (2.0 * w)) for w in (WEIGHTS[1], WEIGHTS[7])}
        out[slot, 0, inner, j * 8 : j * 8 + 8, :] = rest * centre + WEIGHTS[0] * flat
        for n in range(9):
            i = 2 * n + 1
            projection = None
            for step, u in zip(DIRECTIONS[i], (ux, uy, uz)):
                if step == 0:
                    continue
                if projection is None:
                    projection = u
                else:
                    projection = projection + u if step == 1 else projection - u
            level, slope = parts[WEIGHTS[i]]
            odd = slope * projection
            even = level + odd * projection
            plus, minus = both[n]
            out[slot, i, inner, j * 8 : j * 8 + 8, :] = rest * plus + (even + odd)
            out[slot, i + 1, inner, j * 8 : j * 8 + 8, :] = rest * minus + (even - odd)

    loading(0).wait()

    def slab(s, carry):
        slot = lax.rem(s, SLOTS)

        @pl.when(s + 1 < SLABS)
        def _():
            loading(s + 1).wait()

        @pl.when(s >= SLOTS)
        def _():
            storing(s - SLOTS, slot).wait()

        def plane(inner, inside):
            for j in range(WY // 8):
                tile(s * SLAB + inner, j, slot, inner)
            return inside

        lax.fori_loop(0, SLAB, plane, 0, unroll=True)
        storing(s, slot).start()
        return carry

    lax.fori_loop(0, SLABS, slab, 0)
    for s in range(SLABS - SLOTS, SLABS):
        storing(s, s % SLOTS).wait()


def collide(dense_dir, dense_take, low, high, left, right, populations):
    return pl.pallas_call(
        collide_kernel,
        out_shape=jax.ShapeDtypeStruct(populations.shape, jnp.float32),
        in_specs=[whole()] * 6 + [anywhere()],
        out_specs=anywhere(),
        scratch_shapes=[
            pltpu.VMEM((19, WX + 2, WY + 16, NZ), jnp.float32),
            pltpu.VMEM((SLOTS, 19, SLAB, WY, NZ), jnp.float32),
            pltpu.SemaphoreType.DMA((SLABS,)),
            pltpu.SemaphoreType.DMA((SLOTS,)),
        ],
        compiler_params=params(30),
        cost_estimate=cost(40_000_000, 24_000_000),
        name="collide",
    )(dense_dir, dense_take, low, high, left, right, populations)


def fold_kernel(dense, mid, left, right, own, to_low, to_high):
    def total(k):
        rows = slice(k * STATE_ROWS, (k + 1) * STATE_ROWS)
        return mid[rows] + (left[rows] + right[rows])

    to_low[...] = total(0)
    own[...] = total(1)
    to_high[...] = total(2)


def fold(dense, mid, left, right):
    shape = jax.ShapeDtypeStruct((STATE_ROWS, 128), jnp.float32)
    return pl.pallas_call(
        fold_kernel,
        out_shape=(shape,) * 3,
        in_specs=[anywhere(), whole(), whole(), whole()],
        out_specs=(whole(),) * 3,
        compiler_params=params(4),
        cost_estimate=cost(100_000, 600_000),
        name="fold",
    )(dense, mid, left, right)


def motion_kernel(own, low, high, place, velocity, response, out):
    loads = own[...] + low[...] + high[...]
    px, py, pz = origin_terms(place, velocity)
    scale = 1.0 / LEVER_SCALE
    for b in range(GROUPS):
        lanes = slice(b * 128, (b + 1) * 128)

        def load(c):
            return loads[c * GROUPS + b : c * GROUPS + b + 1, :]

        fx, fy, fz = load(0), load(1), load(2)
        qx, qy, qz = px[:, lanes], py[:, lanes], pz[:, lanes]
        torques = [
            load(3) - (qy * fz - qz * fy) * scale,
            load(4) - (qz * fx - qx * fz) * scale,
            load(5) - (qx * fy - qy * fx) * scale,
        ]
        for c, value in enumerate((fx, fy, fz)):
            out[c : c + 1, lanes] = velocity[c : c + 1, lanes] + response[0:1, lanes] * value
        for c, value in enumerate(torques):
            out[c + 3 : c + 4, lanes] = (
                velocity[c + 3 : c + 4, lanes] + response[1:2, lanes] * value
            )


def motion(own, low, high, place, velocity, response):
    return pl.pallas_call(
        motion_kernel,
        out_shape=jax.ShapeDtypeStruct(velocity.shape, jnp.float32),
        in_specs=[whole()] * 6,
        out_specs=whole(),
        compiler_params=params(4),
        cost_estimate=cost(200_000, 300_000),
        name="motion",
    )(own, low, high, place, velocity, response)


def shifted(value, axis, step):
    count = lax.axis_size(axis)
    return lax.ppermute(value, axis, [(i, (i + step) % count) for i in range(count)])


def body(populations, link_cell, link_dir, link_floe, floe_place, floe_velocity, floe_response):
    sizes = (lax.axis_size("along"), lax.axis_size("across"))
    links = link_cell.shape[-1]
    cell = link_cell.reshape(links // 128, 128)
    heading = link_dir.reshape(links // 128, 128)
    floe = link_floe.reshape(links // 128, 128)

    up, down = prepare(floe_place, floe_velocity, populations)
    low = shifted(up, "along", 1)
    high = shifted(down, "along", -1)
    cells, words, work, dense_dir, chosen, face_up, face_down = pick(
        sizes, cell, heading, floe, populations
    )

    def rows(block, k, y):
        at = STATE_ROWS + k * WY + y
        return block[at : at + 1]

    states = [low[:STATE_ROWS], up[:STATE_ROWS], high[:STATE_ROWS]]
    filler = jnp.zeros((EDGE_ROWS - 2, 128), jnp.float32)
    to_up = jnp.concatenate(
        states + [face_up, rows(low, X_UP.index(7), WY - 1), rows(high, X_DOWN.index(10), WY - 1)]
        + [filler]
    )
    to_down = jnp.concatenate(
        states + [face_down, rows(low, X_UP.index(9), 0), rows(high, X_DOWN.index(8), 0), filler]
    )
    left = shifted(to_up, "across", 1)
    right = shifted(to_down, "across", -1)
    here = gather(work, cells, chosen)
    taken, loads_left, loads_mid, loads_right = floes(
        cells, words, here, up, low, high, left, right
    )
    from_right = shifted(loads_left, "across", -1)
    from_left = shifted(loads_right, "across", 1)
    dense_take = spread_out(work, cells, taken)
    own, to_low, to_high = fold(dense_take, loads_mid, from_left, from_right)
    from_high = shifted(to_low, "along", -1)
    from_low = shifted(to_high, "along", 1)
    relaxed = collide(dense_dir, dense_take, low, high, left, right, populations)
    moved = motion(
        own,
        from_low,
        from_high,
        floe_place,
        floe_velocity,
        floe_response,
    )
    return relaxed, moved


def solution(mesh):
    placed = (
        P(None, "along", "across", None),
        P("along", "across", None),
        P("along", "across", None),
        P("along", "across", None),
        P(None, ("along", "across")),
        P(None, ("along", "across")),
        P(None, ("along", "across")),
    )
    return jax.shard_map(
        body,
        mesh=mesh,
        in_specs=placed,
        out_specs=(P(None, "along", "across", None), P(None, ("along", "across"))),
        check_vma=False,
    )
```

```python
import functools

import jax
import jax.numpy as jnp
from jax import lax
from jax.experimental import pallas as pl
from jax.experimental.pallas import tpu as pltpu
from jax.sharding import PartitionSpec as P

DIRECTIONS = [
    (0, 0, 0),
    (0, 0, 1),
    (0, 0, -1),
    (1, 0, 0),
    (-1, 0, 0),
    (0, 1, 0),
    (0, -1, 0),
    (1, 1, 0),
    (-1, -1, 0),
    (1, -1, 0),
    (-1, 1, 0),
    (1, 0, 1),
    (-1, 0, -1),
    (1, 0, -1),
    (-1, 0, 1),
    (0, 1, 1),
    (0, -1, -1),
    (0, 1, -1),
    (0, -1, 1),
]
WEIGHTS = [1.0 / 3.0] + [1.0 / 18.0] * 6 + [1.0 / 36.0] * 12
RELAXATION = 1.0 / 0.6
FLOW_SCALE = 0.02
LEVER_SCALE = 64.0

WX = 32
WY = 32
NZ = 128
COLUMNS = WX * WY
MEMBERS = 2048
GROUPS = MEMBERS // 128
STATE_ROWS = 6 * GROUPS
ROWS_NEAR = 9 * GROUPS
TURNS = 6
HEIGHT = ROWS_NEAR // TURNS
TABLE_ROWS = 6 * HEIGHT
FACE = 5 * WX
EDGE_ROWS = 8
WINDOW = 160
PADDED_COLUMNS = COLUMNS + WINDOW
CHUNK = 1024

X_UP = [i for i in range(19) if DIRECTIONS[i][0] == 1]
X_DOWN = [i for i in range(19) if DIRECTIONS[i][0] == -1]
Y_UP = [i for i in range(19) if DIRECTIONS[i][1] == 1]
Y_DOWN = [i for i in range(19) if DIRECTIONS[i][1] == -1]


def opposite(i):
    if i == 0:
        return 0
    return i + 1 if i % 2 == 1 else i - 1


def params(mebibytes):
    return pltpu.CompilerParams(vmem_limit_bytes=mebibytes * 1024 * 1024)


def cost(flops, moved):
    return pl.CostEstimate(flops=flops, bytes_accessed=moved, transcendentals=0)


def whole():
    return pl.BlockSpec(memory_space=pltpu.VMEM)


def anywhere():
    return pl.BlockSpec(memory_space=pl.ANY)


def origin_terms(place, velocity):
    px = place[0:1] * float(WX)
    py = place[1:2] * float(WY)
    pz = place[2:3] * float(NZ)
    return px, py, pz


def prepare_kernel(
    place_hbm, velocity_hbm, pop, up, down, place, velocity, sem, small_sem
):
    small = [
        pltpu.make_async_copy(place_hbm, place, small_sem.at[0]),
        pltpu.make_async_copy(velocity_hbm, velocity, small_sem.at[1]),
    ]
    for copy in small:
        copy.start()
    copies = []
    for k in range(5):
        rows = pl.ds(STATE_ROWS + k * WY, WY)
        copies.append(pltpu.make_async_copy(pop.at[X_UP[k], WX - 1], up.at[rows, :], sem.at[0]))
        copies.append(pltpu.make_async_copy(pop.at[X_DOWN[k], 0], down.at[rows, :], sem.at[0]))
    for copy in copies:
        copy.start()
    for copy in small:
        copy.wait()
    px, py, pz = origin_terms(place, velocity)
    wx, wy, wz = velocity[3:4], velocity[4:5], velocity[5:6]
    scale = 1.0 / LEVER_SCALE
    values = [
        velocity[0:1] - (wy * pz - wz * py) * scale,
        velocity[1:2] - (wz * px - wx * pz) * scale,
        velocity[2:3] - (wx * py - wy * px) * scale,
        wx,
        wy,
        wz,
    ]
    for c in range(6):
        for b in range(GROUPS):
            row = values[c][:, b * 128 : (b + 1) * 128]
            up[c * GROUPS + b : c * GROUPS + b + 1, :] = row
            down[c * GROUPS + b : c * GROUPS + b + 1, :] = row
    for copy in copies:
        copy.wait()


def prepare(place, velocity, populations):
    shape = jax.ShapeDtypeStruct((STATE_ROWS + FACE, 128), jnp.float32)
    return pl.pallas_call(
        prepare_kernel,
        out_shape=(shape, shape),
        in_specs=[hbm(), hbm(), hbm()],
        out_specs=(whole(),) * 2,
        scratch_shapes=[
            pltpu.VMEM(place.shape, jnp.float32),
            pltpu.VMEM(velocity.shape, jnp.float32),
            pltpu.SemaphoreType.DMA((1,)),
            pltpu.SemaphoreType.DMA((2,)),
        ],
        compiler_params=params(58),
        cost_estimate=cost(100_000, 2_600_000),
        name="prepare",
    )(place, velocity, populations)


NT = (((1,), (1,)), ((), ()))
NN = (((1,), (0,)), ((), ()))


def product(a, b, dims):
    return lax.dot_general(a, b, dims, preferred_element_type=jnp.float32)


def column_hot(cell, start):
    rows = lax.broadcasted_iota(jnp.int32, (WINDOW, cell.shape[1]), 0)
    return jnp.where(rows == jnp.right_shift(cell, 7) - start, 1.0, 0.0).astype(jnp.bfloat16)


def depth_mask(cell):
    rows = lax.broadcasted_iota(jnp.int32, (NZ, cell.shape[1]), 0)
    return rows == jnp.bitwise_and(cell, NZ - 1)


def sorted_chunks(keys, values):
    lane = lax.broadcasted_iota(jnp.int32, (8, 128), 1)
    sublane = lax.broadcasted_iota(jnp.int32, (8, 128), 0)

    def bit(position):
        if position < 6:
            return jnp.bitwise_and(jnp.right_shift(sublane, position - 3), 1)
        return jnp.bitwise_and(jnp.right_shift(lane, position - 6), 1)

    def partner(x, position):
        axis = 0 if position < 6 else 1
        extent = x.shape[axis]
        distance = 1 << (position - (3 if position < 6 else 6))
        if 2 * distance == extent:
            return pltpu.roll(x, distance, axis)
        return jnp.where(
            bit(position) == 0,
            pltpu.roll(x, extent - distance, axis),
            pltpu.roll(x, distance, axis),
        )

    for merge in range(1, 14):
        for position in range(merge - 1, -1, -1):
            if merge == 13 and position < 10:
                continue
            if position < 3:
                for v in range(8):
                    u = v | (1 << position)
                    if u == v:
                        continue
                    below = keys[u] < keys[v]
                    if merge < 3:
                        if (v >> merge) & 1:
                            below = keys[u] > keys[v]
                    elif merge < 13:
                        below = jnp.logical_xor(below, bit(merge) == 1)
                    keys[v], keys[u] = (
                        jnp.where(below, keys[u], keys[v]),
                        jnp.where(below, keys[v], keys[u]),
                    )
                    values[v], values[u] = (
                        jnp.where(below, values[u], values[v]),
                        jnp.where(below, values[v], values[u]),
                    )
                continue
            if merge < 13:
                least = bit(position) == bit(merge)
            else:
                least = bit(position) == 0
            for v in range(8):
                other = partner(keys[v], position)
                carried = partner(values[v], position)
                stay = jnp.logical_xor(other < keys[v], least)
                keys[v] = jnp.where(stay, keys[v], other)
                values[v] = jnp.where(stay, values[v], carried)
    return keys, values


def pick_kernel(
    sizes, cell, heading, floe, pop, cells, words, work, dense, chosen, face_up, face_down,
    turned, resident, sem,
):
    load = pltpu.make_async_copy(pop, resident, sem.at[0])
    load.start()
    size_along, size_across = sizes
    a = lax.axis_index("along")
    b = lax.axis_index("across")
    keys = []
    values = []
    for v in range(8):
        rows = slice(v * 8, (v + 1) * 8)
        g = floe[rows, :]
        owner = jnp.right_shift(g, 11)
        ra = jnp.bitwise_and(owner // size_across - a + 1, size_along - 1)
        rb = jnp.bitwise_and(jnp.bitwise_and(owner, size_across - 1) - b + 1, size_across - 1)
        entry = (ra * 3 + rb) * MEMBERS + jnp.bitwise_and(g, MEMBERS - 1)
        word = jnp.left_shift(heading[rows, :], 15) + entry
        keys.append(cell[rows, :])
        values.append(jnp.where(g >= 0, word, 9 * MEMBERS))
    keys, values = sorted_chunks(keys, values)
    turned[...] = jnp.transpose(jnp.concatenate(keys + values, axis=0))
    even = turned[pl.ds(0, 64, stride=2), :]
    odd = turned[pl.ds(1, 64, stride=2), :]
    left = lax.broadcasted_iota(jnp.int32, (64, 128), 1) < 64
    key = jnp.where(left, even, pltpu.roll(odd, 64, 1))
    value = jnp.where(left, pltpu.roll(even, 64, 1), odd)
    for r in range(64):
        cells[:, r * 128 : (r + 1) * 128] = key[r : r + 1, :]
        words[:, r * 128 : (r + 1) * 128] = value[r : r + 1, :]
    column = jnp.right_shift(key, 7)
    count = jnp.int32(8)
    for c in range(8):
        part = column[c * 8 : (c + 1) * 8, :]
        first = jnp.left_shift(jnp.right_shift(jnp.min(part), 3), 3)
        last = jnp.max(part)
        windows = (last - first) // WINDOW + 1
        work[0, c] = c
        work[1, c] = first

        def enter(w, n, c=c, first=first):
            work[0, n] = c
            work[1, n] = first + w * WINDOW
            return n + 1

        count = lax.fori_loop(1, windows, enter, count)
    work[2, 0] = count
    dense[...] = jnp.zeros_like(dense)

    def scatter(at, start):
        own = cells[:, at]
        kind = jnp.right_shift(words[:, at], 15).astype(jnp.float32)
        payload = jnp.where(depth_mask(own), kind, 0.0).astype(jnp.bfloat16)
        return product(column_hot(own, start), payload, NT)

    over_windows(work, scatter, window_adder(dense))
    load.wait()
    for k in range(5):
        face_up[k * WX : (k + 1) * WX, :] = resident[Y_UP[k], :, WY - 1, :]
        face_down[k * WX : (k + 1) * WX, :] = resident[Y_DOWN[k], :, 0, :]
    chosen[COLUMNS:] = jnp.zeros((PADDED_COLUMNS - COLUMNS, NZ), jnp.float32)

    def select(x, carry):
        rows = pl.ds(pl.multiple_of(x * WY, WY), WY)
        where = dense[rows, :]
        value = jnp.zeros((WY, NZ), jnp.float32)
        for i in range(1, 19):
            value = jnp.where(where == float(i), resident[i, x], value)
        chosen[rows, :] = value
        return carry

    lax.fori_loop(0, WX, select, 0, unroll=2)


def window_adder(dense):
    def add(at, start, value):
        dense[pl.ds(start, WINDOW), :] += value

    return add


def over_windows(work, compute, apply):
    for group in range(0, 8, 4):
        results = []
        for c in range(group, group + 4):
            at = slice(c * 1024, (c + 1) * 1024)
            start = pl.multiple_of(work[1, c], 8)
            results.append((at, start, compute(at, start)))
        for result in results:
            apply(*result)

    def step(n, carry):
        at = pl.ds(pl.multiple_of(work[0, n] * 1024, 1024), 1024)
        start = pl.multiple_of(work[1, n], 8)
        apply(at, start, compute(at, start))
        return carry

    lax.fori_loop(8, work[2, 0], step, 0)


def hbm():
    return pl.BlockSpec(memory_space=pltpu.HBM)


def smem():
    return pl.BlockSpec(memory_space=pltpu.SMEM)


def pick(sizes, cell, heading, floe, populations):
    links = cell.shape[0] * cell.shape[1]
    face = jax.ShapeDtypeStruct((FACE, 128), jnp.float32)
    row = jax.ShapeDtypeStruct((1, links), jnp.int32)
    return pl.pallas_call(
        functools.partial(pick_kernel, sizes),
        out_shape=(
            row,
            row,
            jax.ShapeDtypeStruct((3, 32), jnp.int32),
            jax.ShapeDtypeStruct((PADDED_COLUMNS, NZ), jnp.float32),
            jax.ShapeDtypeStruct((PADDED_COLUMNS, NZ), jnp.float32),
            face,
            face,
        ),
        in_specs=[whole(), whole(), whole(), hbm()],
        out_specs=(whole(), whole(), smem(), whole(), whole(), whole(), whole()),
        scratch_shapes=[
            pltpu.VMEM((128, 128), jnp.int32),
            pltpu.VMEM(populations.shape, jnp.float32),
            pltpu.SemaphoreType.DMA((1,)),
        ],
        compiler_params=params(48),
        cost_estimate=cost(7_000_000_000, 1_000_000),
        name="pick",
    )(cell, heading, floe, populations)


def gather_kernel(work, cell, chosen, out):
    out[...] = jnp.zeros_like(out)

    def read(at, start):
        own = cell[:, at]
        turned = jnp.transpose(chosen[pl.ds(start, WINDOW), :])
        high = turned.astype(jnp.bfloat16)
        low = (turned - high.astype(jnp.float32)).astype(jnp.bfloat16)
        values = product(jnp.concatenate([high, low], axis=0), column_hot(own, start), NN)
        values = values[0:NZ] + values[NZ : 2 * NZ]
        return jnp.sum(jnp.where(depth_mask(own), values, 0.0), axis=0, keepdims=True)

    def add(at, start, value):
        out[:, at] += value

    over_windows(work, read, add)


def gather(work, cell, chosen):
    return pl.pallas_call(
        gather_kernel,
        out_shape=jax.ShapeDtypeStruct(cell.shape, jnp.float32),
        in_specs=[smem(), whole(), whole()],
        out_specs=whole(),
        compiler_params=params(12),
        cost_estimate=cost(6_000_000_000, 2_000_000),
        name="gather",
    )(work, cell, chosen)


def bits(table, heading):
    word = 0
    for i in table:
        word |= 1 << i
    return jnp.bitwise_and(jnp.right_shift(jnp.full_like(heading, word), heading), 1)


def component(axis, heading):
    plus = [i for i in range(19) if DIRECTIONS[i][axis] == 1]
    minus = [i for i in range(19) if DIRECTIONS[i][axis] == -1]
    return (bits(plus, heading) - bits(minus, heading)).astype(jnp.float32)


def floe_kernel(
    cell, words, here, mine, low, high, left, right,
    taken, loads_left, loads_mid, loads_right, near, flat, table, hot, spread, payload, total,
):
    links = cell.shape[1]
    for ra in range(3):
        for rb in range(3):
            if rb == 0:
                state = left[ra * STATE_ROWS : (ra + 1) * STATE_ROWS]
            elif rb == 2:
                state = right[ra * STATE_ROWS : (ra + 1) * STATE_ROWS]
            else:
                state = (low, mine, high)[ra][0:STATE_ROWS]
            first_row = (ra * 3 + rb) * GROUPS
            for c in range(6):
                near[c * ROWS_NEAR + first_row : c * ROWS_NEAR + first_row + GROUPS] = state[
                    c * GROUPS : (c + 1) * GROUPS
                ]
    for c in range(6):
        for q in range(TURNS):
            flat[c * HEIGHT : (c + 1) * HEIGHT, q * 128 : (q + 1) * 128] = near[
                pl.ds(c * ROWS_NEAR + q, HEIGHT, stride=TURNS), :
            ]
    whole_table = flat[...]
    top = whole_table.astype(jnp.bfloat16)
    table[0:TABLE_ROWS] = top
    table[TABLE_ROWS : 2 * TABLE_ROWS] = (whole_table - top.astype(jnp.float32)).astype(
        jnp.bfloat16
    )

    def first_half(t):
        slot = t % 2
        at = slice(t * CHUNK, (t + 1) * CHUNK)
        k = cell[:, at]
        word = words[:, at]
        d = jnp.right_shift(word, 15)
        place = jnp.bitwise_and(word, 32767)
        region = jnp.right_shift(place, 11)
        ra = jnp.right_shift(region * 11, 5)
        rb = region - 3 * ra
        near_row = jnp.right_shift(place, 7)
        group = jnp.right_shift(near_row * 171, 10)
        entry = (near_row - TURNS * group) * 128 + jnp.bitwise_and(place, 127)
        rows = lax.broadcasted_iota(jnp.int32, (TURNS * 128, CHUNK), 0)
        pick_floe = jnp.where(rows == entry, 1.0, 0.0).astype(jnp.bfloat16)
        groups = lax.broadcasted_iota(jnp.int32, (HEIGHT, CHUNK), 0)
        mask = jnp.where(groups == group, 1.0, 0.0)

        cx = component(0, d)
        cy = component(1, d)
        cz = component(2, d)
        weight = jnp.where(d <= 6, WEIGHTS[1], WEIGHTS[7])
        lx = jnp.right_shift(k, 12)
        ly = jnp.bitwise_and(jnp.right_shift(k, 7), 31)
        lz = jnp.bitwise_and(k, 127)
        rx = ((1 - ra) * WX + lx).astype(jnp.float32) + 0.5 * cx
        ry = ((1 - rb) * WY + ly).astype(jnp.float32) + 0.5 * cy
        rz = lz.astype(jnp.float32) + 0.5 * cz
        scale = 1.0 / LEVER_SCALE
        coefficients = [
            cx,
            cy,
            cz,
            (ry * cz - rz * cy) * scale,
            (rz * cx - rx * cz) * scale,
            (rx * cy - ry * cx) * scale,
        ]
        for c in range(6):
            spread[slot, c * HEIGHT : (c + 1) * HEIGHT, :] = mask * coefficients[c]
        hot[slot] = pick_floe

        state = product(table[...], pick_floe, NN)
        state = state[0:TABLE_ROWS] + state[TABLE_ROWS : 2 * TABLE_ROWS]
        weights = spread[slot]
        speed = jnp.sum(state * weights, axis=0, keepdims=True)
        take = (6.0 * FLOW_SCALE) * weight * speed
        magnitude = 2.0 * here[:, at] - take
        taken[:, at] = take
        amount = weights * magnitude
        first = amount.astype(jnp.bfloat16)
        payload[slot, 0:TABLE_ROWS, :] = first
        payload[slot, TABLE_ROWS : 2 * TABLE_ROWS, :] = (amount - first.astype(jnp.float32)).astype(
            jnp.bfloat16
        )

    def second_half(t):
        value = product(payload[t % 2], hot[t % 2], NT)
        if t == 0:
            total[...] = value
        else:
            total[...] += value

    steps = links // CHUNK
    first_half(0)
    for t in range(1, steps):
        first_half(t)
        second_half(t - 1)
    second_half(steps - 1)
    flat[...] = total[0:TABLE_ROWS] + total[TABLE_ROWS : 2 * TABLE_ROWS]
    for c in range(6):
        for q in range(TURNS):
            near[pl.ds(c * ROWS_NEAR + q, HEIGHT, stride=TURNS), :] = flat[
                c * HEIGHT : (c + 1) * HEIGHT, q * 128 : (q + 1) * 128
            ]
    for ra in range(3):
        for rb in range(3):
            out = (loads_left, loads_mid, loads_right)[rb]
            first_row = (ra * 3 + rb) * GROUPS
            for c in range(6):
                at = ra * STATE_ROWS + c * GROUPS
                out[at : at + GROUPS] = near[
                    c * ROWS_NEAR + first_row : c * ROWS_NEAR + first_row + GROUPS
                ]


def floes(cell, words, here, mine, low, high, left, right):
    loads = jax.ShapeDtypeStruct((3 * STATE_ROWS, 128), jnp.float32)
    return pl.pallas_call(
        floe_kernel,
        out_shape=(jax.ShapeDtypeStruct(cell.shape, jnp.float32), loads, loads, loads),
        in_specs=[whole()] * 8,
        out_specs=(whole(),) * 4,
        scratch_shapes=[
            pltpu.VMEM((6 * ROWS_NEAR, 128), jnp.float32),
            pltpu.VMEM((TABLE_ROWS, TURNS * 128), jnp.float32),
            pltpu.VMEM((2 * TABLE_ROWS, TURNS * 128), jnp.bfloat16),
            pltpu.VMEM((2, TURNS * 128, CHUNK), jnp.bfloat16),
            pltpu.VMEM((2, TABLE_ROWS, CHUNK), jnp.float32),
            pltpu.VMEM((2, 2 * TABLE_ROWS, CHUNK), jnp.bfloat16),
            pltpu.VMEM((2 * TABLE_ROWS, TURNS * 128), jnp.float32),
        ],
        compiler_params=params(18),
        cost_estimate=cost(8_000_000_000, 2_000_000),
        name="floes",
    )(cell, words, here, mine, low, high, left, right)


def spread_kernel(work, cell, taken, dense):
    dense[...] = jnp.zeros_like(dense)

    def scatter(at, start):
        own = cell[:, at]
        value = taken[:, at]
        first = value.astype(jnp.bfloat16).astype(jnp.float32)
        mask = depth_mask(own)
        payload = jnp.concatenate(
            [
                jnp.where(mask, first, 0.0).astype(jnp.bfloat16),
                jnp.where(mask, value - first, 0.0).astype(jnp.bfloat16),
            ],
            axis=0,
        )
        both = product(column_hot(own, start), payload, NT)
        return both[:, :NZ] + both[:, NZ:]

    over_windows(work, scatter, window_adder(dense))


def spread_out(work, cell, taken):
    return pl.pallas_call(
        spread_kernel,
        out_shape=jax.ShapeDtypeStruct((PADDED_COLUMNS, NZ), jnp.float32),
        in_specs=[smem(), whole(), whole()],
        out_specs=whole(),
        compiler_params=params(8),
        cost_estimate=cost(3_000_000_000, 1_000_000),
        name="spread",
    )(work, cell, taken)


SLAB = 2
SLOTS = 4
SLABS = WX // SLAB
TOP = 8


def collide_kernel(
    dense_dir, dense_take, low, high, left, right, pop_hbm, out_hbm, pop, out, load_sem, store_sem
):
    def loading(s):
        return pltpu.make_async_copy(
            pop_hbm.at[:, pl.ds(s * SLAB, SLAB)],
            pop.at[:, pl.ds(1 + s * SLAB, SLAB), pl.ds(TOP, WY), :],
            load_sem.at[s],
        )

    for s in range(SLABS):
        loading(s).start()
    for k in range(5):
        rows = slice(STATE_ROWS + k * WY, STATE_ROWS + (k + 1) * WY)
        pop[X_UP[k], 0, TOP : TOP + WY, :] = low[rows, :]
        pop[X_DOWN[k], WX + 1, TOP : TOP + WY, :] = high[rows, :]
    base = 3 * STATE_ROWS
    for k in range(5):
        for x in range(WX):
            row = base + k * WX + x
            pop[Y_UP[k], 1 + x, TOP - 1 : TOP, :] = left[row : row + 1, :]
            pop[Y_DOWN[k], 1 + x, TOP + WY : TOP + WY + 1, :] = right[row : row + 1, :]
    edge = base + FACE
    pop[7, 0, TOP - 1 : TOP, :] = left[edge : edge + 1, :]
    pop[10, WX + 1, TOP - 1 : TOP, :] = left[edge + 1 : edge + 2, :]
    pop[9, 0, TOP + WY : TOP + WY + 1, :] = right[edge : edge + 1, :]
    pop[8, WX + 1, TOP + WY : TOP + WY + 1, :] = right[edge + 1 : edge + 2, :]

    def storing(s, slot):
        return pltpu.make_async_copy(
            out.at[slot], out_hbm.at[:, pl.ds(s * SLAB, SLAB)], store_sem.at[slot]
        )

    lane = lax.broadcasted_iota(jnp.int32, (8, 128), 1)
    first_lane = lane == 0
    last_lane = lane == NZ - 1
    rest = 1.0 - RELAXATION

    def tile(x, j, slot, inner):
        row = pl.multiple_of(x * WY, WY) + j * 8
        where = dense_dir[pl.ds(row, 8), :]
        take = dense_take[pl.ds(row, 8), :]

        def plain(i):
            return pop[i, x + 1, TOP + j * 8 : TOP + j * 8 + 8, :]

        def bounded(i, back):
            step_x, step_y, step_z = DIRECTIONS[i]
            start = TOP + j * 8 - step_y
            value = pop[i, x + 1 - step_x, start : start + 8, :]
            if step_z == 1:
                value = jnp.where(first_lane, back, pltpu.roll(value, 1, 1))
            elif step_z == -1:
                value = jnp.where(last_lane, back, pltpu.roll(value, NZ - 1, 1))
            return jnp.where(where == float(opposite(i)), back - take, value)

        centre = plain(0)
        density = centre
        both = []
        apart = []
        for i in range(1, 19, 2):
            plus = bounded(i, plain(i + 1))
            minus = bounded(i + 1, plain(i))
            both.append((plus, minus))
            apart.append(plus - minus)
            density = density + (plus + minus)
        d1, d3, d5, d7, d9, d11, d13, d15, d17 = apart
        mx = (d3 + d7) + (d9 + d11) + d13
        my = (d5 + d7) + (d15 - d9) + d17
        mz = (d1 + d11) + (d15 - d13) - d17
        inverse = 1.5 / density
        ux = mx * inverse
        uy = my * inverse
        uz = mz * inverse
        scaled = density * RELAXATION
        flat = scaled - (2.0 / 3.0) * scaled * (ux * ux + uy * uy + uz * uz)
        parts = {w: (flat * w, scaled * (2.0 * w)) for w in (WEIGHTS[1], WEIGHTS[7])}
        out[slot, 0, inner, j * 8 : j * 8 + 8, :] = rest * centre + WEIGHTS[0] * flat
        for n in range(9):
            i = 2 * n + 1
            projection = None
            for step, u in zip(DIRECTIONS[i], (ux, uy, uz)):
                if step == 0:
                    continue
                if projection is None:
                    projection = u
                else:
                    projection = projection + u if step == 1 else projection - u
            level, slope = parts[WEIGHTS[i]]
            odd = slope * projection
            even = level + odd * projection
            plus, minus = both[n]
            out[slot, i, inner, j * 8 : j * 8 + 8, :] = rest * plus + (even + odd)
            out[slot, i + 1, inner, j * 8 : j * 8 + 8, :] = rest * minus + (even - odd)

    loading(0).wait()

    def slab(s, carry):
        slot = lax.rem(s, SLOTS)

        @pl.when(s + 1 < SLABS)
        def _():
            loading(s + 1).wait()

        @pl.when(s >= SLOTS)
        def _():
            storing(s - SLOTS, slot).wait()

        def plane(inner, inside):
            for j in range(WY // 8):
                tile(s * SLAB + inner, j, slot, inner)
            return inside

        lax.fori_loop(0, SLAB, plane, 0, unroll=True)
        storing(s, slot).start()
        return carry

    lax.fori_loop(0, SLABS, slab, 0)
    for s in range(SLABS - SLOTS, SLABS):
        storing(s, s % SLOTS).wait()


def collide(dense_dir, dense_take, low, high, left, right, populations):
    return pl.pallas_call(
        collide_kernel,
        out_shape=jax.ShapeDtypeStruct(populations.shape, jnp.float32),
        in_specs=[whole()] * 6 + [anywhere()],
        out_specs=anywhere(),
        scratch_shapes=[
            pltpu.VMEM((19, WX + 2, WY + 16, NZ), jnp.float32),
            pltpu.VMEM((SLOTS, 19, SLAB, WY, NZ), jnp.float32),
            pltpu.SemaphoreType.DMA((SLABS,)),
            pltpu.SemaphoreType.DMA((SLOTS,)),
        ],
        compiler_params=params(30),
        cost_estimate=cost(40_000_000, 24_000_000),
        name="collide",
    )(dense_dir, dense_take, low, high, left, right, populations)


def fold_kernel(dense, mid, left, right, own, to_low, to_high):
    def total(k):
        rows = slice(k * STATE_ROWS, (k + 1) * STATE_ROWS)
        return mid[rows] + (left[rows] + right[rows])

    to_low[...] = total(0)
    own[...] = total(1)
    to_high[...] = total(2)


def fold(dense, mid, left, right):
    shape = jax.ShapeDtypeStruct((STATE_ROWS, 128), jnp.float32)
    return pl.pallas_call(
        fold_kernel,
        out_shape=(shape,) * 3,
        in_specs=[anywhere(), whole(), whole(), whole()],
        out_specs=(whole(),) * 3,
        compiler_params=params(4),
        cost_estimate=cost(100_000, 600_000),
        name="fold",
    )(dense, mid, left, right)


def motion_kernel(own, low, high, place, velocity, response, out):
    loads = own[...] + low[...] + high[...]
    px, py, pz = origin_terms(place, velocity)
    scale = 1.0 / LEVER_SCALE
    for b in range(GROUPS):
        lanes = slice(b * 128, (b + 1) * 128)

        def load(c):
            return loads[c * GROUPS + b : c * GROUPS + b + 1, :]

        fx, fy, fz = load(0), load(1), load(2)
        qx, qy, qz = px[:, lanes], py[:, lanes], pz[:, lanes]
        torques = [
            load(3) - (qy * fz - qz * fy) * scale,
            load(4) - (qz * fx - qx * fz) * scale,
            load(5) - (qx * fy - qy * fx) * scale,
        ]
        for c, value in enumerate((fx, fy, fz)):
            out[c : c + 1, lanes] = velocity[c : c + 1, lanes] + response[0:1, lanes] * value
        for c, value in enumerate(torques):
            out[c + 3 : c + 4, lanes] = (
                velocity[c + 3 : c + 4, lanes] + response[1:2, lanes] * value
            )


def motion(own, low, high, place, velocity, response):
    return pl.pallas_call(
        motion_kernel,
        out_shape=jax.ShapeDtypeStruct(velocity.shape, jnp.float32),
        in_specs=[whole()] * 6,
        out_specs=whole(),
        compiler_params=params(4),
        cost_estimate=cost(200_000, 300_000),
        name="motion",
    )(own, low, high, place, velocity, response)


def shifted(value, axis, step):
    count = lax.axis_size(axis)
    return lax.ppermute(value, axis, [(i, (i + step) % count) for i in range(count)])


def body(populations, link_cell, link_dir, link_floe, floe_place, floe_velocity, floe_response):
    sizes = (lax.axis_size("along"), lax.axis_size("across"))
    links = link_cell.shape[-1]
    cell = link_cell.reshape(links // 128, 128)
    heading = link_dir.reshape(links // 128, 128)
    floe = link_floe.reshape(links // 128, 128)

    up, down = prepare(floe_place, floe_velocity, populations)
    low = shifted(up, "along", 1)
    high = shifted(down, "along", -1)
    cells, words, work, dense_dir, chosen, face_up, face_down = pick(
        sizes, cell, heading, floe, populations
    )

    def rows(block, k, y):
        at = STATE_ROWS + k * WY + y
        return block[at : at + 1]

    states = [low[:STATE_ROWS], up[:STATE_ROWS], high[:STATE_ROWS]]
    filler = jnp.zeros((EDGE_ROWS - 2, 128), jnp.float32)
    to_up = jnp.concatenate(
        states + [face_up, rows(low, X_UP.index(7), WY - 1), rows(high, X_DOWN.index(10), WY - 1)]
        + [filler]
    )
    to_down = jnp.concatenate(
        states + [face_down, rows(low, X_UP.index(9), 0), rows(high, X_DOWN.index(8), 0), filler]
    )
    left = shifted(to_up, "across", 1)
    right = shifted(to_down, "across", -1)
    here = gather(work, cells, chosen)
    taken, loads_left, loads_mid, loads_right = floes(
        cells, words, here, up, low, high, left, right
    )
    from_right = shifted(loads_left, "across", -1)
    from_left = shifted(loads_right, "across", 1)
    dense_take = spread_out(work, cells, taken)
    own, to_low, to_high = fold(dense_take, loads_mid, from_left, from_right)
    from_high = shifted(to_low, "along", -1)
    from_low = shifted(to_high, "along", 1)
    relaxed = collide(dense_dir, dense_take, low, high, left, right, populations)
    moved = motion(
        own,
        from_low,
        from_high,
        floe_place,
        floe_velocity,
        floe_response,
    )
    return relaxed, moved


def solution(mesh):
    placed = (
        P(None, "along", "across", None),
        P("along", "across", None),
        P("along", "across", None),
        P("along", "across", None),
        P(None, ("along", "across")),
        P(None, ("along", "across")),
        P(None, ("along", "across")),
    )
    return jax.shard_map(
        body,
        mesh=mesh,
        in_specs=placed,
        out_specs=(P(None, "along", "across", None), P(None, ("along", "across"))),
        check_vma=False,
    )
```

```python
import functools

import jax
import jax.numpy as jnp
from jax import lax
from jax.experimental import pallas as pl
from jax.experimental.pallas import tpu as pltpu
from jax.sharding import PartitionSpec as P

DIRECTIONS = [
    (0, 0, 0),
    (0, 0, 1),
    (0, 0, -1),
    (1, 0, 0),
    (-1, 0, 0),
    (0, 1, 0),
    (0, -1, 0),
    (1, 1, 0),
    (-1, -1, 0),
    (1, -1, 0),
    (-1, 1, 0),
    (1, 0, 1),
    (-1, 0, -1),
    (1, 0, -1),
    (-1, 0, 1),
    (0, 1, 1),
    (0, -1, -1),
    (0, 1, -1),
    (0, -1, 1),
]
WEIGHTS = [1.0 / 3.0] + [1.0 / 18.0] * 6 + [1.0 / 36.0] * 12
RELAXATION = 1.0 / 0.6
FLOW_SCALE = 0.02
LEVER_SCALE = 64.0

WX = 32
WY = 32
NZ = 128
COLUMNS = WX * WY
MEMBERS = 2048
GROUPS = MEMBERS // 128
STATE_ROWS = 6 * GROUPS
ROWS_NEAR = 9 * GROUPS
TURNS = 6
HEIGHT = ROWS_NEAR // TURNS
TABLE_ROWS = 6 * HEIGHT
FACE = 5 * WX
EDGE_ROWS = 8
WINDOW = 160
PADDED_COLUMNS = COLUMNS + WINDOW
CHUNK = 1024

X_UP = [i for i in range(19) if DIRECTIONS[i][0] == 1]
X_DOWN = [i for i in range(19) if DIRECTIONS[i][0] == -1]
Y_UP = [i for i in range(19) if DIRECTIONS[i][1] == 1]
Y_DOWN = [i for i in range(19) if DIRECTIONS[i][1] == -1]


def opposite(i):
    if i == 0:
        return 0
    return i + 1 if i % 2 == 1 else i - 1


def params(mebibytes):
    return pltpu.CompilerParams(vmem_limit_bytes=mebibytes * 1024 * 1024)


def cost(flops, moved):
    return pl.CostEstimate(flops=flops, bytes_accessed=moved, transcendentals=0)


def whole():
    return pl.BlockSpec(memory_space=pltpu.VMEM)


def anywhere():
    return pl.BlockSpec(memory_space=pl.ANY)


def origin_terms(place, velocity):
    px = place[0:1] * float(WX)
    py = place[1:2] * float(WY)
    pz = place[2:3] * float(NZ)
    return px, py, pz


def prepare_kernel(
    place_hbm, velocity_hbm, pop, up, down, place, velocity, sem, small_sem
):
    small = [
        pltpu.make_async_copy(place_hbm, place, small_sem.at[0]),
        pltpu.make_async_copy(velocity_hbm, velocity, small_sem.at[1]),
    ]
    for copy in small:
        copy.start()
    copies = []
    for k in range(5):
        rows = pl.ds(STATE_ROWS + k * WY, WY)
        copies.append(pltpu.make_async_copy(pop.at[X_UP[k], WX - 1], up.at[rows, :], sem.at[0]))
        copies.append(pltpu.make_async_copy(pop.at[X_DOWN[k], 0], down.at[rows, :], sem.at[0]))
    for copy in copies:
        copy.start()
    for copy in small:
        copy.wait()
    px, py, pz = origin_terms(place, velocity)
    wx, wy, wz = velocity[3:4], velocity[4:5], velocity[5:6]
    scale = 1.0 / LEVER_SCALE
    values = [
        velocity[0:1] - (wy * pz - wz * py) * scale,
        velocity[1:2] - (wz * px - wx * pz) * scale,
        velocity[2:3] - (wx * py - wy * px) * scale,
        wx,
        wy,
        wz,
    ]
    for c in range(6):
        for b in range(GROUPS):
            row = values[c][:, b * 128 : (b + 1) * 128]
            up[c * GROUPS + b : c * GROUPS + b + 1, :] = row
            down[c * GROUPS + b : c * GROUPS + b + 1, :] = row
    for copy in copies:
        copy.wait()


def prepare(place, velocity, populations):
    shape = jax.ShapeDtypeStruct((STATE_ROWS + FACE, 128), jnp.float32)
    return pl.pallas_call(
        prepare_kernel,
        out_shape=(shape, shape),
        in_specs=[hbm(), hbm(), hbm()],
        out_specs=(whole(),) * 2,
        scratch_shapes=[
            pltpu.VMEM(place.shape, jnp.float32),
            pltpu.VMEM(velocity.shape, jnp.float32),
            pltpu.SemaphoreType.DMA((1,)),
            pltpu.SemaphoreType.DMA((2,)),
        ],
        compiler_params=params(58),
        cost_estimate=cost(100_000, 2_600_000),
        name="prepare",
    )(place, velocity, populations)


NT = (((1,), (1,)), ((), ()))
NN = (((1,), (0,)), ((), ()))


def product(a, b, dims):
    return lax.dot_general(a, b, dims, preferred_element_type=jnp.float32)


def column_hot(cell, start):
    rows = lax.broadcasted_iota(jnp.int32, (WINDOW, cell.shape[1]), 0)
    return jnp.where(rows == jnp.right_shift(cell, 7) - start, 1.0, 0.0).astype(jnp.bfloat16)


def depth_mask(cell):
    rows = lax.broadcasted_iota(jnp.int32, (NZ, cell.shape[1]), 0)
    return rows == jnp.bitwise_and(cell, NZ - 1)


def sorted_chunks(keys, values):
    lane = lax.broadcasted_iota(jnp.int32, (8, 128), 1)
    sublane = lax.broadcasted_iota(jnp.int32, (8, 128), 0)

    def bit(position):
        if position < 6:
            return jnp.bitwise_and(jnp.right_shift(sublane, position - 3), 1)
        return jnp.bitwise_and(jnp.right_shift(lane, position - 6), 1)

    def partner(x, position):
        axis = 0 if position < 6 else 1
        extent = x.shape[axis]
        distance = 1 << (position - (3 if position < 6 else 6))
        if 2 * distance == extent:
            return pltpu.roll(x, distance, axis)
        return jnp.where(
            bit(position) == 0,
            pltpu.roll(x, extent - distance, axis),
            pltpu.roll(x, distance, axis),
        )

    for merge in range(1, 14):
        for position in range(merge - 1, -1, -1):
            if merge == 13 and position < 10:
                continue
            if position < 3:
                for v in range(8):
                    u = v | (1 << position)
                    if u == v:
                        continue
                    below = keys[u] < keys[v]
                    if merge < 3:
                        if (v >> merge) & 1:
                            below = keys[u] > keys[v]
                    elif merge < 13:
                        below = jnp.logical_xor(below, bit(merge) == 1)
                    keys[v], keys[u] = (
                        jnp.where(below, keys[u], keys[v]),
                        jnp.where(below, keys[v], keys[u]),
                    )
                    values[v], values[u] = (
                        jnp.where(below, values[u], values[v]),
                        jnp.where(below, values[v], values[u]),
                    )
                continue
            if merge < 13:
                least = bit(position) == bit(merge)
            else:
                least = bit(position) == 0
            for v in range(8):
                other = partner(keys[v], position)
                carried = partner(values[v], position)
                stay = jnp.logical_xor(other < keys[v], least)
                keys[v] = jnp.where(stay, keys[v], other)
                values[v] = jnp.where(stay, values[v], carried)
    return keys, values


def pick_kernel(
    sizes, cell, heading, floe, pop, cells, words, work, dense, chosen, face_up, face_down,
    turned, resident, sem,
):
    load = pltpu.make_async_copy(pop, resident, sem.at[0])
    load.start()
    size_along, size_across = sizes
    a = lax.axis_index("along")
    b = lax.axis_index("across")
    keys = []
    values = []
    for v in range(8):
        rows = slice(v * 8, (v + 1) * 8)
        g = floe[rows, :]
        owner = jnp.right_shift(g, 11)
        ra = jnp.bitwise_and(owner // size_across - a + 1, size_along - 1)
        rb = jnp.bitwise_and(jnp.bitwise_and(owner, size_across - 1) - b + 1, size_across - 1)
        entry = (ra * 3 + rb) * MEMBERS + jnp.bitwise_and(g, MEMBERS - 1)
        word = jnp.left_shift(heading[rows, :], 15) + entry
        keys.append(cell[rows, :])
        values.append(jnp.where(g >= 0, word, 9 * MEMBERS))
    keys, values = sorted_chunks(keys, values)
    turned[...] = jnp.transpose(jnp.concatenate(keys + values, axis=0))
    even = turned[pl.ds(0, 64, stride=2), :]
    odd = turned[pl.ds(1, 64, stride=2), :]
    left = lax.broadcasted_iota(jnp.int32, (64, 128), 1) < 64
    key = jnp.where(left, even, pltpu.roll(odd, 64, 1))
    value = jnp.where(left, pltpu.roll(even, 64, 1), odd)
    for r in range(64):
        cells[:, r * 128 : (r + 1) * 128] = key[r : r + 1, :]
        words[:, r * 128 : (r + 1) * 128] = value[r : r + 1, :]
    column = jnp.right_shift(key, 7)
    count = jnp.int32(8)
    for c in range(8):
        part = column[c * 8 : (c + 1) * 8, :]
        first = jnp.left_shift(jnp.right_shift(jnp.min(part), 3), 3)
        last = jnp.max(part)
        windows = (last - first) // WINDOW + 1
        work[0, c] = c
        work[1, c] = first

        def enter(w, n, c=c, first=first):
            work[0, n] = c
            work[1, n] = first + w * WINDOW
            return n + 1

        count = lax.fori_loop(1, windows, enter, count)
    work[2, 0] = count
    dense[...] = jnp.zeros_like(dense)

    def scatter(at, start):
        own = cells[:, at]
        kind = jnp.right_shift(words[:, at], 15).astype(jnp.float32)
        payload = jnp.where(depth_mask(own), kind, 0.0).astype(jnp.bfloat16)
        return product(column_hot(own, start), payload, NT)

    over_windows(work, scatter, window_adder(dense))
    load.wait()
    for k in range(5):
        face_up[k * WX : (k + 1) * WX, :] = resident[Y_UP[k], :, WY - 1, :]
        face_down[k * WX : (k + 1) * WX, :] = resident[Y_DOWN[k], :, 0, :]
    chosen[COLUMNS:] = jnp.zeros((PADDED_COLUMNS - COLUMNS, NZ), jnp.float32)

    def select(x, carry):
        rows = pl.ds(pl.multiple_of(x * WY, WY), WY)
        where = dense[rows, :]
        value = jnp.zeros((WY, NZ), jnp.float32)
        for i in range(1, 19):
            value = jnp.where(where == float(i), resident[i, x], value)
        chosen[rows, :] = value
        return carry

    lax.fori_loop(0, WX, select, 0, unroll=8)


def window_adder(dense):
    def add(at, start, value):
        dense[pl.ds(start, WINDOW), :] += value

    return add


def over_windows(work, compute, apply):
    for group in range(0, 8, 4):
        results = []
        for c in range(group, group + 4):
            at = slice(c * 1024, (c + 1) * 1024)
            start = pl.multiple_of(work[1, c], 8)
            results.append((at, start, compute(at, start)))
        for result in results:
            apply(*result)

    def step(n, carry):
        at = pl.ds(pl.multiple_of(work[0, n] * 1024, 1024), 1024)
        start = pl.multiple_of(work[1, n], 8)
        apply(at, start, compute(at, start))
        return carry

    lax.fori_loop(8, work[2, 0], step, 0)


def hbm():
    return pl.BlockSpec(memory_space=pltpu.HBM)


def smem():
    return pl.BlockSpec(memory_space=pltpu.SMEM)


def pick(sizes, cell, heading, floe, populations):
    links = cell.shape[0] * cell.shape[1]
    face = jax.ShapeDtypeStruct((FACE, 128), jnp.float32)
    row = jax.ShapeDtypeStruct((1, links), jnp.int32)
    return pl.pallas_call(
        functools.partial(pick_kernel, sizes),
        out_shape=(
            row,
            row,
            jax.ShapeDtypeStruct((3, 32), jnp.int32),
            jax.ShapeDtypeStruct((PADDED_COLUMNS, NZ), jnp.float32),
            jax.ShapeDtypeStruct((PADDED_COLUMNS, NZ), jnp.float32),
            face,
            face,
        ),
        in_specs=[whole(), whole(), whole(), hbm()],
        out_specs=(whole(), whole(), smem(), whole(), whole(), whole(), whole()),
        scratch_shapes=[
            pltpu.VMEM((128, 128), jnp.int32),
            pltpu.VMEM(populations.shape, jnp.float32),
            pltpu.SemaphoreType.DMA((1,)),
        ],
        compiler_params=params(48),
        cost_estimate=cost(7_000_000_000, 1_000_000),
        name="pick",
    )(cell, heading, floe, populations)


def gather_kernel(work, cell, chosen, out):
    out[...] = jnp.zeros_like(out)

    def read(at, start):
        own = cell[:, at]
        turned = jnp.transpose(chosen[pl.ds(start, WINDOW), :])
        high = turned.astype(jnp.bfloat16)
        low = (turned - high.astype(jnp.float32)).astype(jnp.bfloat16)
        values = product(jnp.concatenate([high, low], axis=0), column_hot(own, start), NN)
        values = values[0:NZ] + values[NZ : 2 * NZ]
        return jnp.sum(jnp.where(depth_mask(own), values, 0.0), axis=0, keepdims=True)

    def add(at, start, value):
        out[:, at] += value

    over_windows(work, read, add)


def gather(work, cell, chosen):
    return pl.pallas_call(
        gather_kernel,
        out_shape=jax.ShapeDtypeStruct(cell.shape, jnp.float32),
        in_specs=[smem(), whole(), whole()],
        out_specs=whole(),
        compiler_params=params(12),
        cost_estimate=cost(6_000_000_000, 2_000_000),
        name="gather",
    )(work, cell, chosen)


def bits(table, heading):
    word = 0
    for i in table:
        word |= 1 << i
    return jnp.bitwise_and(jnp.right_shift(jnp.full_like(heading, word), heading), 1)


def component(axis, heading):
    plus = [i for i in range(19) if DIRECTIONS[i][axis] == 1]
    minus = [i for i in range(19) if DIRECTIONS[i][axis] == -1]
    return (bits(plus, heading) - bits(minus, heading)).astype(jnp.float32)


def floe_kernel(
    cell, words, here, mine, low, high, left, right,
    taken, loads_left, loads_mid, loads_right, near, flat, table, hot, spread, payload, total,
):
    links = cell.shape[1]
    for ra in range(3):
        for rb in range(3):
            if rb == 0:
                state = left[ra * STATE_ROWS : (ra + 1) * STATE_ROWS]
            elif rb == 2:
                state = right[ra * STATE_ROWS : (ra + 1) * STATE_ROWS]
            else:
                state = (low, mine, high)[ra][0:STATE_ROWS]
            first_row = (ra * 3 + rb) * GROUPS
            for c in range(6):
                near[c * ROWS_NEAR + first_row : c * ROWS_NEAR + first_row + GROUPS] = state[
                    c * GROUPS : (c + 1) * GROUPS
                ]
    for c in range(6):
        for q in range(TURNS):
            flat[c * HEIGHT : (c + 1) * HEIGHT, q * 128 : (q + 1) * 128] = near[
                pl.ds(c * ROWS_NEAR + q, HEIGHT, stride=TURNS), :
            ]
    whole_table = flat[...]
    top = whole_table.astype(jnp.bfloat16)
    table[0:TABLE_ROWS] = top
    table[TABLE_ROWS : 2 * TABLE_ROWS] = (whole_table - top.astype(jnp.float32)).astype(
        jnp.bfloat16
    )

    def first_half(t):
        slot = t % 2
        at = slice(t * CHUNK, (t + 1) * CHUNK)
        k = cell[:, at]
        word = words[:, at]
        d = jnp.right_shift(word, 15)
        place = jnp.bitwise_and(word, 32767)
        region = jnp.right_shift(place, 11)
        ra = jnp.right_shift(region * 11, 5)
        rb = region - 3 * ra
        near_row = jnp.right_shift(place, 7)
        group = jnp.right_shift(near_row * 171, 10)
        entry = (near_row - TURNS * group) * 128 + jnp.bitwise_and(place, 127)
        rows = lax.broadcasted_iota(jnp.int32, (TURNS * 128, CHUNK), 0)
        pick_floe = jnp.where(rows == entry, 1.0, 0.0).astype(jnp.bfloat16)
        groups = lax.broadcasted_iota(jnp.int32, (HEIGHT, CHUNK), 0)
        mask = jnp.where(groups == group, 1.0, 0.0)

        cx = component(0, d)
        cy = component(1, d)
        cz = component(2, d)
        weight = jnp.where(d <= 6, WEIGHTS[1], WEIGHTS[7])
        lx = jnp.right_shift(k, 12)
        ly = jnp.bitwise_and(jnp.right_shift(k, 7), 31)
        lz = jnp.bitwise_and(k, 127)
        rx = ((1 - ra) * WX + lx).astype(jnp.float32) + 0.5 * cx
        ry = ((1 - rb) * WY + ly).astype(jnp.float32) + 0.5 * cy
        rz = lz.astype(jnp.float32) + 0.5 * cz
        scale = 1.0 / LEVER_SCALE
        coefficients = [
            cx,
            cy,
            cz,
            (ry * cz - rz * cy) * scale,
            (rz * cx - rx * cz) * scale,
            (rx * cy - ry * cx) * scale,
        ]
        for c in range(6):
            spread[slot, c * HEIGHT : (c + 1) * HEIGHT, :] = mask * coefficients[c]
        hot[slot] = pick_floe

        state = product(table[...], pick_floe, NN)
        state = state[0:TABLE_ROWS] + state[TABLE_ROWS : 2 * TABLE_ROWS]
        weights = spread[slot]
        speed = jnp.sum(state * weights, axis=0, keepdims=True)
        take = (6.0 * FLOW_SCALE) * weight * speed
        magnitude = 2.0 * here[:, at] - take
        taken[:, at] = take
        amount = weights * magnitude
        first = amount.astype(jnp.bfloat16)
        payload[slot, 0:TABLE_ROWS, :] = first
        payload[slot, TABLE_ROWS : 2 * TABLE_ROWS, :] = (amount - first.astype(jnp.float32)).astype(
            jnp.bfloat16
        )

    def second_half(t):
        value = product(payload[t % 2], hot[t % 2], NT)
        if t == 0:
            total[...] = value
        else:
            total[...] += value

    steps = links // CHUNK
    first_half(0)
    for t in range(1, steps):
        first_half(t)
        second_half(t - 1)
    second_half(steps - 1)
    flat[...] = total[0:TABLE_ROWS] + total[TABLE_ROWS : 2 * TABLE_ROWS]
    for c in range(6):
        for q in range(TURNS):
            near[pl.ds(c * ROWS_NEAR + q, HEIGHT, stride=TURNS), :] = flat[
                c * HEIGHT : (c + 1) * HEIGHT, q * 128 : (q + 1) * 128
            ]
    for ra in range(3):
        for rb in range(3):
            out = (loads_left, loads_mid, loads_right)[rb]
            first_row = (ra * 3 + rb) * GROUPS
            for c in range(6):
                at = ra * STATE_ROWS + c * GROUPS
                out[at : at + GROUPS] = near[
                    c * ROWS_NEAR + first_row : c * ROWS_NEAR + first_row + GROUPS
                ]


def floes(cell, words, here, mine, low, high, left, right):
    loads = jax.ShapeDtypeStruct((3 * STATE_ROWS, 128), jnp.float32)
    return pl.pallas_call(
        floe_kernel,
        out_shape=(jax.ShapeDtypeStruct(cell.shape, jnp.float32), loads, loads, loads),
        in_specs=[whole()] * 8,
        out_specs=(whole(),) * 4,
        scratch_shapes=[
            pltpu.VMEM((6 * ROWS_NEAR, 128), jnp.float32),
            pltpu.VMEM((TABLE_ROWS, TURNS * 128), jnp.float32),
            pltpu.VMEM((2 * TABLE_ROWS, TURNS * 128), jnp.bfloat16),
            pltpu.VMEM((2, TURNS * 128, CHUNK), jnp.bfloat16),
            pltpu.VMEM((2, TABLE_ROWS, CHUNK), jnp.float32),
            pltpu.VMEM((2, 2 * TABLE_ROWS, CHUNK), jnp.bfloat16),
            pltpu.VMEM((2 * TABLE_ROWS, TURNS * 128), jnp.float32),
        ],
        compiler_params=params(18),
        cost_estimate=cost(8_000_000_000, 2_000_000),
        name="floes",
    )(cell, words, here, mine, low, high, left, right)


def spread_kernel(work, cell, taken, dense):
    dense[...] = jnp.zeros_like(dense)

    def scatter(at, start):
        own = cell[:, at]
        value = taken[:, at]
        first = value.astype(jnp.bfloat16).astype(jnp.float32)
        mask = depth_mask(own)
        payload = jnp.concatenate(
            [
                jnp.where(mask, first, 0.0).astype(jnp.bfloat16),
                jnp.where(mask, value - first, 0.0).astype(jnp.bfloat16),
            ],
            axis=0,
        )
        both = product(column_hot(own, start), payload, NT)
        return both[:, :NZ] + both[:, NZ:]

    over_windows(work, scatter, window_adder(dense))


def spread_out(work, cell, taken):
    return pl.pallas_call(
        spread_kernel,
        out_shape=jax.ShapeDtypeStruct((PADDED_COLUMNS, NZ), jnp.float32),
        in_specs=[smem(), whole(), whole()],
        out_specs=whole(),
        compiler_params=params(8),
        cost_estimate=cost(3_000_000_000, 1_000_000),
        name="spread",
    )(work, cell, taken)


SLAB = 2
SLOTS = 4
SLABS = WX // SLAB
TOP = 8


def collide_kernel(
    dense_dir, dense_take, low, high, left, right, pop_hbm, out_hbm, pop, out, load_sem, store_sem
):
    def loading(s):
        return pltpu.make_async_copy(
            pop_hbm.at[:, pl.ds(s * SLAB, SLAB)],
            pop.at[:, pl.ds(1 + s * SLAB, SLAB), pl.ds(TOP, WY), :],
            load_sem.at[s],
        )

    for s in range(SLABS):
        loading(s).start()
    for k in range(5):
        rows = slice(STATE_ROWS + k * WY, STATE_ROWS + (k + 1) * WY)
        pop[X_UP[k], 0, TOP : TOP + WY, :] = low[rows, :]
        pop[X_DOWN[k], WX + 1, TOP : TOP + WY, :] = high[rows, :]
    base = 3 * STATE_ROWS
    for k in range(5):
        for x in range(WX):
            row = base + k * WX + x
            pop[Y_UP[k], 1 + x, TOP - 1 : TOP, :] = left[row : row + 1, :]
            pop[Y_DOWN[k], 1 + x, TOP + WY : TOP + WY + 1, :] = right[row : row + 1, :]
    edge = base + FACE
    pop[7, 0, TOP - 1 : TOP, :] = left[edge : edge + 1, :]
    pop[10, WX + 1, TOP - 1 : TOP, :] = left[edge + 1 : edge + 2, :]
    pop[9, 0, TOP + WY : TOP + WY + 1, :] = right[edge : edge + 1, :]
    pop[8, WX + 1, TOP + WY : TOP + WY + 1, :] = right[edge + 1 : edge + 2, :]

    def storing(s, slot):
        return pltpu.make_async_copy(
            out.at[slot], out_hbm.at[:, pl.ds(s * SLAB, SLAB)], store_sem.at[slot]
        )

    lane = lax.broadcasted_iota(jnp.int32, (8, 128), 1)
    first_lane = lane == 0
    last_lane = lane == NZ - 1
    rest = 1.0 - RELAXATION

    def tile(x, j, slot, inner):
        row = pl.multiple_of(x * WY, WY) + j * 8
        where = dense_dir[pl.ds(row, 8), :]
        take = dense_take[pl.ds(row, 8), :]

        def plain(i):
            return pop[i, x + 1, TOP + j * 8 : TOP + j * 8 + 8, :]

        def bounded(i, back):
            step_x, step_y, step_z = DIRECTIONS[i]
            start = TOP + j * 8 - step_y
            value = pop[i, x + 1 - step_x, start : start + 8, :]
            if step_z == 1:
                value = jnp.where(first_lane, back, pltpu.roll(value, 1, 1))
            elif step_z == -1:
                value = jnp.where(last_lane, back, pltpu.roll(value, NZ - 1, 1))
            return jnp.where(where == float(opposite(i)), back - take, value)

        centre = plain(0)
        density = centre
        both = []
        apart = []
        for i in range(1, 19, 2):
            plus = bounded(i, plain(i + 1))
            minus = bounded(i + 1, plain(i))
            both.append((plus, minus))
            apart.append(plus - minus)
            density = density + (plus + minus)
        d1, d3, d5, d7, d9, d11, d13, d15, d17 = apart
        mx = (d3 + d7) + (d9 + d11) + d13
        my = (d5 + d7) + (d15 - d9) + d17
        mz = (d1 + d11) + (d15 - d13) - d17
        inverse = 1.5 / density
        ux = mx * inverse
        uy = my * inverse
        uz = mz * inverse
        scaled = density * RELAXATION
        flat = scaled - (2.0 / 3.0) * scaled * (ux * ux + uy * uy + uz * uz)
        parts = {w: (flat * w, scaled * (2.0 * w)) for w in (WEIGHTS[1], WEIGHTS[7])}
        out[slot, 0, inner, j * 8 : j * 8 + 8, :] = rest * centre + WEIGHTS[0] * flat
        for n in range(9):
            i = 2 * n + 1
            projection = None
            for step, u in zip(DIRECTIONS[i], (ux, uy, uz)):
                if step == 0:
                    continue
                if projection is None:
                    projection = u
                else:
                    projection = projection + u if step == 1 else projection - u
            level, slope = parts[WEIGHTS[i]]
            odd = slope * projection
            even = level + odd * projection
            plus, minus = both[n]
            out[slot, i, inner, j * 8 : j * 8 + 8, :] = rest * plus + (even + odd)
            out[slot, i + 1, inner, j * 8 : j * 8 + 8, :] = rest * minus + (even - odd)

    loading(0).wait()

    def slab(s, carry):
        slot = lax.rem(s, SLOTS)

        @pl.when(s + 1 < SLABS)
        def _():
            loading(s + 1).wait()

        @pl.when(s >= SLOTS)
        def _():
            storing(s - SLOTS, slot).wait()

        def plane(inner, inside):
            for j in range(WY // 8):
                tile(s * SLAB + inner, j, slot, inner)
            return inside

        lax.fori_loop(0, SLAB, plane, 0, unroll=True)
        storing(s, slot).start()
        return carry

    lax.fori_loop(0, SLABS, slab, 0)
    for s in range(SLABS - SLOTS, SLABS):
        storing(s, s % SLOTS).wait()


def collide(dense_dir, dense_take, low, high, left, right, populations):
    return pl.pallas_call(
        collide_kernel,
        out_shape=jax.ShapeDtypeStruct(populations.shape, jnp.float32),
        in_specs=[whole()] * 6 + [anywhere()],
        out_specs=anywhere(),
        scratch_shapes=[
            pltpu.VMEM((19, WX + 2, WY + 16, NZ), jnp.float32),
            pltpu.VMEM((SLOTS, 19, SLAB, WY, NZ), jnp.float32),
            pltpu.SemaphoreType.DMA((SLABS,)),
            pltpu.SemaphoreType.DMA((SLOTS,)),
        ],
        compiler_params=params(30),
        cost_estimate=cost(40_000_000, 24_000_000),
        name="collide",
    )(dense_dir, dense_take, low, high, left, right, populations)


def fold_kernel(dense, mid, left, right, own, to_low, to_high):
    def total(k):
        rows = slice(k * STATE_ROWS, (k + 1) * STATE_ROWS)
        return mid[rows] + (left[rows] + right[rows])

    to_low[...] = total(0)
    own[...] = total(1)
    to_high[...] = total(2)


def fold(dense, mid, left, right):
    shape = jax.ShapeDtypeStruct((STATE_ROWS, 128), jnp.float32)
    return pl.pallas_call(
        fold_kernel,
        out_shape=(shape,) * 3,
        in_specs=[anywhere(), whole(), whole(), whole()],
        out_specs=(whole(),) * 3,
        compiler_params=params(4),
        cost_estimate=cost(100_000, 600_000),
        name="fold",
    )(dense, mid, left, right)


def motion_kernel(own, low, high, place, velocity, response, out):
    loads = own[...] + low[...] + high[...]
    px, py, pz = origin_terms(place, velocity)
    scale = 1.0 / LEVER_SCALE
    for b in range(GROUPS):
        lanes = slice(b * 128, (b + 1) * 128)

        def load(c):
            return loads[c * GROUPS + b : c * GROUPS + b + 1, :]

        fx, fy, fz = load(0), load(1), load(2)
        qx, qy, qz = px[:, lanes], py[:, lanes], pz[:, lanes]
        torques = [
            load(3) - (qy * fz - qz * fy) * scale,
            load(4) - (qz * fx - qx * fz) * scale,
            load(5) - (qx * fy - qy * fx) * scale,
        ]
        for c, value in enumerate((fx, fy, fz)):
            out[c : c + 1, lanes] = velocity[c : c + 1, lanes] + response[0:1, lanes] * value
        for c, value in enumerate(torques):
            out[c + 3 : c + 4, lanes] = (
                velocity[c + 3 : c + 4, lanes] + response[1:2, lanes] * value
            )


def motion(own, low, high, place, velocity, response):
    return pl.pallas_call(
        motion_kernel,
        out_shape=jax.ShapeDtypeStruct(velocity.shape, jnp.float32),
        in_specs=[whole()] * 6,
        out_specs=whole(),
        compiler_params=params(4),
        cost_estimate=cost(200_000, 300_000),
        name="motion",
    )(own, low, high, place, velocity, response)


def shifted(value, axis, step):
    count = lax.axis_size(axis)
    return lax.ppermute(value, axis, [(i, (i + step) % count) for i in range(count)])


def body(populations, link_cell, link_dir, link_floe, floe_place, floe_velocity, floe_response):
    sizes = (lax.axis_size("along"), lax.axis_size("across"))
    links = link_cell.shape[-1]
    cell = link_cell.reshape(links // 128, 128)
    heading = link_dir.reshape(links // 128, 128)
    floe = link_floe.reshape(links // 128, 128)

    up, down = prepare(floe_place, floe_velocity, populations)
    low = shifted(up, "along", 1)
    high = shifted(down, "along", -1)
    cells, words, work, dense_dir, chosen, face_up, face_down = pick(
        sizes, cell, heading, floe, populations
    )

    def rows(block, k, y):
        at = STATE_ROWS + k * WY + y
        return block[at : at + 1]

    states = [low[:STATE_ROWS], up[:STATE_ROWS], high[:STATE_ROWS]]
    filler = jnp.zeros((EDGE_ROWS - 2, 128), jnp.float32)
    to_up = jnp.concatenate(
        states + [face_up, rows(low, X_UP.index(7), WY - 1), rows(high, X_DOWN.index(10), WY - 1)]
        + [filler]
    )
    to_down = jnp.concatenate(
        states + [face_down, rows(low, X_UP.index(9), 0), rows(high, X_DOWN.index(8), 0), filler]
    )
    left = shifted(to_up, "across", 1)
    right = shifted(to_down, "across", -1)
    here = gather(work, cells, chosen)
    taken, loads_left, loads_mid, loads_right = floes(
        cells, words, here, up, low, high, left, right
    )
    from_right = shifted(loads_left, "across", -1)
    from_left = shifted(loads_right, "across", 1)
    dense_take = spread_out(work, cells, taken)
    own, to_low, to_high = fold(dense_take, loads_mid, from_left, from_right)
    from_high = shifted(to_low, "along", -1)
    from_low = shifted(to_high, "along", 1)
    relaxed = collide(dense_dir, dense_take, low, high, left, right, populations)
    moved = motion(
        own,
        from_low,
        from_high,
        floe_place,
        floe_velocity,
        floe_response,
    )
    return relaxed, moved


def solution(mesh):
    placed = (
        P(None, "along", "across", None),
        P("along", "across", None),
        P("along", "across", None),
        P("along", "across", None),
        P(None, ("along", "across")),
        P(None, ("along", "across")),
        P(None, ("along", "across")),
    )
    return jax.shard_map(
        body,
        mesh=mesh,
        in_specs=placed,
        out_specs=(P(None, "along", "across", None), P(None, ("along", "across"))),
        check_vma=False,
    )
```
